128 devices in a mesh: dp: 32 (over x_hi, y, z), tensor: 4 (over x_lo, core).
Axes of the slice: x: 4 (x_hi: 2, x_lo: 2; x = x_hi * 2 + x_lo), y: 4, z: 4, core: 2. Of those that a mesh axis runs over, the one named last changes fastest.
Arguments:
- tokens: bfloat16 [1024, 8192], P('dp', 'tensor'), may hold values from -6 to 6
- out_grad: bfloat16 [1024, 8192], P('dp', 'tensor'), may hold values from -6 to 6
- gate_weight: bfloat16 [8192, 28672], P('tensor', 'dp'), may hold values from -0.0625 to 0.0625
- up_weight: bfloat16 [8192, 28672], P('tensor', 'dp'), may hold values from -0.0625 to 0.0625
- down_weight: bfloat16 [28672, 8192], P('dp', 'tensor'), may hold values from -0.0625 to 0.0625
- pocket_ids: int32 [1024], replicated, may hold values from 0 to 15, never falling along the last dimension, each value on 1 to 341 neighbouring positions
Outputs:
- act_cov: float32 [8192, 8192], P('tensor', 'dp')
- grad_cov: float32 [8192, 8192], P('tensor', 'dp')
- hidden_cov: float32 [28672, 1024], P(('dp', 'tensor'))
- gate_grad_cov: float32 [28672, 1024], P(('dp', 'tensor'))
- up_grad_cov: float32 [28672, 1024], P(('dp', 'tensor'))
The draws below stay inside these ranges and needn't reach their ends.
Inputs may be any that keep to these rules, and one draw needn't show every extreme that they name: `pocket_ids`: pocket ids never fall along the tokens, every one of the 16 pockets holds at least one token and at most 341, and one holds exactly 341.
All inputs are finite; a program needn't handle non-finite values.
Results may differ from the reference program's by a relative error of at most 0.0043.
Values may be sent and summed in bfloat16 or wider, within the bound.
A program may use at most 192 MiB of HBM per device.

```python
import math
import jax
import jax.numpy as jnp
import numpy as np
from jax import lax

D = 8192
FF = 28672
BLOCK = 1024
POCKETS = 16
TOKENS = 1024
POCKET_MOST = 341


def block_levels(key, shape, pieces, least, top_value):
    loudness = 1.0
    for dim, blocks in pieces:
        steps = jax.random.uniform(jax.random.fold_in(jax.random.fold_in(key, 6), dim), (blocks,), jnp.float32, least / len(pieces), top_value / len(pieces))
        loudness = loudness * jnp.repeat(jnp.exp(steps), shape[dim] // blocks).reshape((-1,) + (1,) * (len(shape) - 1 - dim))
    return loudness


def length_profile(amount, total, limit, slope):
    weights = [(1 << 20) // math.isqrt(rank ** slope) + 1 for rank in range(2, amount + 1)]
    rest, given = total - limit - (amount - 1), [1] * (amount - 1)
    while rest > 0:
        free = [i for i in range(amount - 1) if given[i] < limit]
        pool, budget = sum([weights[i] for i in free]), rest
        for i in free:
            extra = min(limit - given[i], max(1, budget * weights[i] // pool), rest)
            given[i] = given[i] + extra
            rest = rest - extra
    return np.array([limit] + given)


def ragged_sizes(own_key, amount, total, reach, skew):
    if amount == 2:
        one = jax.random.randint(own_key, (), max(1, total - reach), min(reach, total - 1) + 1)
        return jnp.stack([one, total - one])
    lengths = jnp.asarray(length_profile(amount, total, reach, skew), jnp.int32)
    pairs = (amount - 1) // 2
    giver, taker = lengths[1:1 + 2 * pairs:2], lengths[2:2 + 2 * pairs:2]
    room = jnp.minimum(giver - 1, reach - taker)
    shifted = jax.random.randint(jax.random.fold_in(own_key, 1), (pairs,), 0, 1 << 20) % (room + 1)
    lengths = lengths.at[1:1 + 2 * pairs:2].set(giver - shifted).at[2:2 + 2 * pairs:2].set(taker + shifted)
    return lengths[jax.random.permutation(jax.random.fold_in(own_key, 2), amount)]


def noise(rng, extent, scale, bound, pieces=(), kind=jnp.bfloat16):
    drawn = scale * jax.random.normal(rng, extent, jnp.float32)
    if pieces:
        drawn = drawn * block_levels(rng, extent, pieces, -0.22, 0.18)
    return jnp.clip(drawn, -bound, bound).astype(kind)


def setup_inputs(seed: int = 0) -> dict:
    key_of = jax.random.split(jax.random.key(seed), 7)
    tokens = noise(key_of[0], (TOKENS, D), 1.0, 6.0, ((0, 32), (1, 4)))
    out_grad = noise(key_of[1], (TOKENS, D), 1.0, 6.0, ((0, 32), (1, 4)))
    gate_weight = noise(key_of[2], (D, FF), D ** -0.5, 0.0625, ((0, 4), (1, 32)))
    up_weight = noise(key_of[3], (D, FF), D ** -0.5, 0.0625, ((0, 4), (1, 32)))
    down_weight = noise(key_of[4], (FF, D), D ** -0.5, 0.0625, ((0, 32), (1, 4)))
    pocket_ids = jnp.searchsorted(jnp.cumsum(ragged_sizes(key_of[5], POCKETS, TOKENS, POCKET_MOST, 2)), jnp.arange(TOKENS), side="right").astype(jnp.int32)
    return {"tokens": tokens, "out_grad": out_grad, "gate_weight": gate_weight, "up_weight": up_weight, "down_weight": down_weight, "pocket_ids": pocket_ids}


def pocket_weights(pocket_ids):
    membership = (pocket_ids[:, None] == jnp.arange(POCKETS, dtype=jnp.int32)[None, :]).astype(jnp.float32)
    counts = jnp.sum(membership, axis=0)
    pocket_share = 1.0 / (POCKETS * counts)
    return jnp.sum(membership * pocket_share[None, :], axis=1)


def blockwise(values, weights):
    scaled = (values * weights[:, None]).astype(jnp.bfloat16)
    left = scaled.astype(jnp.float32).reshape(TOKENS, FF // BLOCK, BLOCK)
    right = values.astype(jnp.float32).reshape(TOKENS, FF // BLOCK, BLOCK)
    result = jnp.einsum("tbi,tbj->bij", left, right, precision=lax.Precision.HIGHEST)
    return result.reshape(FF, BLOCK)


def full_cov(values, weights):
    scaled = (values * weights[:, None]).astype(jnp.bfloat16)
    return lax.dot_general(scaled, values, (((0,), (0,)), ((), ())), preferred_element_type=jnp.float32)


def reference(tokens, out_grad, gate_weight, up_weight, down_weight, pocket_ids):
    weights = pocket_weights(pocket_ids)
    gate_proj = jnp.dot(tokens, gate_weight, preferred_element_type=jnp.float32)
    up_proj = jnp.dot(tokens, up_weight, preferred_element_type=jnp.float32)
    back_proj = jnp.dot(out_grad, down_weight.T, preferred_element_type=jnp.float32)
    sigmoid_gate = jax.nn.sigmoid(gate_proj)
    activated = gate_proj * sigmoid_gate
    hidden = (activated * up_proj).astype(jnp.bfloat16)
    gate_grad = (back_proj * up_proj * sigmoid_gate * (1.0 + gate_proj * (1.0 - sigmoid_gate))).astype(jnp.bfloat16)
    up_grad = (back_proj * activated).astype(jnp.bfloat16)
    act_cov = full_cov(tokens, weights)
    grad_cov = full_cov(out_grad, weights)
    return (act_cov, grad_cov, blockwise(hidden, weights), blockwise(gate_grad, weights), blockwise(up_grad, weights))
```

```python
import functools

import jax
import jax.numpy as jnp
from jax import lax
from jax.experimental import pallas as pl
from jax.experimental.pallas import tpu as pltpu
from jax.sharding import PartitionSpec as P

MESH = pl.DeviceIdType.MESH
POCKETS = 16
BF = jnp.bfloat16
F32 = jnp.float32
MIB = 1 << 20
CHUNKS = 4
UNITS = 224
SLICE = 896
PIECE = 128
GATE, UP, BACK = 0, 1, 2
LEVELS = 32767.0
TINY = 1e-30


def mod4(v):
    return lax.rem(v + 4, 4)


class Sems:
    def __init__(self, ref):
        self.ref, self.used = ref, 0

    def take(self, count=1):
        base = self.used
        self.used += count
        return base


def kernel(
    tok, grd, gate_h, up_h, down_h, ids_ref,
    act_o, grad_o, hid_o, gg_o, ug_o,
    xt, wg, wu, wd, pbuf, rbuf, xsend, xrecv, tsend, trecv, vw, sb, cols, wrow, wcol,
    ssem, rsem, lsem,
):
    dp = lax.axis_index("dp")
    tensor = lax.axis_index("tensor")
    xh, y, z = dp // 16, (dp // 4) % 4, dp % 4
    xl, c = tensor // 2, tensor % 2
    e = dp % 8

    def dev(xh_, y_, z_, xl_, c_):
        return {"dp": xh_ * 16 + y_ * 4 + z_, "tensor": xl_ * 2 + c_}

    sibling = dev(xh, y, z, xl, 1 - c)
    partner = dev(xh, y, z, 1 - xl, c)
    twin = dev(1 - xh, y, z, xl, c)
    y_peer = [dev(xh, mod4(y + s), z, xl, c) for s in (1, 2, 3)]
    z_peer = [dev(xh, y, mod4(z + s), xl, c) for s in (1, 2, 3)]
    above = {"dp": lax.rem(dp + 1, 32), "tensor": tensor}
    below = {"dp": lax.rem(dp + 31, 32), "tensor": tensor}
    across = [dev(1 - xh, y, z, 1 - xl, k) for k in (0, 1)]

    send, recv, here = Sems(ssem), Sems(rsem), Sems(lsem)
    unsent = []

    def push(src, dst, to, r=None):
        s = send.take()
        r = recv.take() if r is None else r
        copy = pltpu.make_async_remote_copy(
            src_ref=src, dst_ref=dst, send_sem=ssem.at[s], recv_sem=rsem.at[r],
            device_id=to, device_id_type=MESH,
        )
        copy.start()
        unsent.append(copy.wait_send)
        return r

    def arrived(ref, r):
        pltpu.make_async_copy(ref, ref, rsem.at[r]).wait()

    def stay(src, dst):
        copy = pltpu.make_async_copy(src, dst, lsem.at[here.take()])
        copy.start()
        return copy

    shard = (tok, grd)
    pkg_of = (y, 4 + z)
    inner = (xh * 64 + z * 16, xh * 64 + y * 16)
    twin_inner = ((1 - xh) * 64 + z * 16, (1 - xh) * 64 + y * 16)

    def rows16(ref, a, half, start):
        return ref.at[a, pkg_of[half], pl.ds(pl.multiple_of(start, 16), 16)]

    own_copies = [
        [stay(shard[a].at[pl.ds(16 * h, 16)], rows16(xt, a, h, inner[h])) for h in (0, 1)]
        for a in (0, 1)
    ]
    weight_copies = [stay(gate_h, wg), stay(up_h, wu), stay(down_h, wd)]

    barrier = pltpu.get_barrier_semaphore()
    greeted = [sibling, partner, twin, *y_peer, *z_peer, above, below, *across]
    for peer in greeted:
        pl.semaphore_signal(barrier, inc=1, device_id=peer, device_id_type=MESH)
    pl.semaphore_wait(barrier, len(greeted))

    twin_sem = [[recv.take() for _ in (0, 1)] for _ in (0, 1)]
    ring_sem = [[recv.take() for _ in (0, 1)] for _ in (0, 1)]
    ring_peer = (z_peer, y_peer)
    def start_twin(a):
        for h in (0, 1):
            push(shard[a].at[pl.ds(16 * h, 16)], rows16(xt, a, h, inner[h]), twin, twin_sem[a][h])

    def start_ring(a):
        for h in (0, 1):
            for peer in ring_peer[h]:
                push(shard[a].at[pl.ds(16 * h, 16)], rows16(xt, a, h, inner[h]), peer, ring_sem[a][h])

    def forward_twin(a):
        for h in (0, 1):
            piece = rows16(xt, a, h, twin_inner[h])
            arrived(piece, twin_sem[a][h])
            for peer in ring_peer[h]:
                push(piece, piece, peer, ring_sem[a][h])

    side_peer = ((y_peer[2], y_peer[0]), (z_peer[2], z_peer[0]))
    side_sem = [[[recv.take() for _ in (0, 1)] for _ in (0, 1)] for _ in (0, 1)]
    far_sem = [[[recv.take() for _ in (0, 1)] for _ in (0, 1)] for _ in (0, 1)]
    coord = (y, z)

    def package(h, step):
        return 4 * h + mod4(coord[h] + step)

    def send_packages(a):
        for h in (0, 1):
            own_copies[a][h].wait()
            arrived(xt.at[a, pkg_of[h], pl.ds(0, 96)], ring_sem[a][h])
            whole = xt.at[a, pkg_of[h]]
            for s in (0, 1):
                push(whole, whole, side_peer[h][s], side_sem[a][h][1 - s])

    def forward_packages(a):
        for h in (0, 1):
            for s in (0, 1):
                whole = xt.at[a, package(h, (-1, 1)[s])]
                arrived(whole, side_sem[a][h][s])
                part = xt.at[a, package(h, (-1, 1)[s]), pl.ds(64 * s, 64)]
                push(part, part, side_peer[h][1 - s], far_sem[a][h][s])

    def far_packages(a):
        for h in (0, 1):
            for s in (0, 1):
                arrived(xt.at[a, package(h, 2), pl.ds(64 * s, 64)], far_sem[a][h][s])

    chunk_pkgs = [
        (package(0, 0), package(1, 0)),
        (package(0, -1), package(0, 1)),
        (package(1, -1), package(1, 1)),
        (package(0, 2), package(1, 2)),
    ]

    def pkgs_of(k, y_, z_):
        return [
            (y_, 4 + z_),
            (mod4(y_ - 1), mod4(y_ + 1)),
            (4 + mod4(z_ - 1), 4 + mod4(z_ + 1)),
            (mod4(y_ + 2), 4 + mod4(z_ + 2)),
        ][k]

    core_sem = [[recv.take() for _ in range(3)] for _ in range(CHUNKS)]
    line_sem = [[recv.take() for _ in range(3)] for _ in range(CHUNKS)]
    top_sem = [[recv.take() for _ in range(3)] for _ in range(CHUNKS)]
    slot_of = {}
    slot_sent = [None] * 3
    weights_in = [False] * 3

    def project(k, m):
        if not weights_in[m]:
            weight_copies[m].wait()
            weights_in[m] = True
        slot = len(slot_of) % 3
        assert (k, m, slot) not in slot_of and not any(v == slot for v in busy.values())
        a = 1 if m == BACK else 0
        x = jnp.concatenate([xt[a, chunk_pkgs[k][0]], xt[a, chunk_pkgs[k][1]]], axis=0)
        if m == BACK:
            part = lax.dot_general(wd[...], x, (((1,), (1,)), ((), ())), preferred_element_type=F32)
        else:
            w = (wg, wu)[m]
            part = lax.dot_general(w[...], x, (((0,), (1,)), ((), ())), preferred_element_type=F32)
        if slot_sent[slot] is not None:
            slot_sent[slot]()
        for i in range(4):
            pbuf[slot, i // 2, i % 2] = part[UNITS * i : UNITS * (i + 1)]
        push(pbuf.at[slot, :, 1 - c], rbuf.at[k, m], sibling, core_sem[k][m])
        slot_sent[slot] = unsent.pop()
        slot_of[k, m] = slot
        busy[k, m] = slot

    busy = {}

    def combine(k, m):
        slot = busy.pop((k, m))
        arrived(rbuf.at[k, m], core_sem[k][m])

        def add(i, top):
            r = pl.ds(pl.multiple_of(i * 32, 32), 32)
            value = rbuf[k, m, 1 - xl, r] + pbuf[slot, 1 - xl, c, r]
            rbuf[k, m, 1 - xl, r] = value
            rbuf[k, m, xl, r] = rbuf[k, m, xl, r] + pbuf[slot, xl, c, r]
            return jnp.maximum(top, jnp.abs(value))

        top = lax.fori_loop(0, UNITS // 32, add, jnp.zeros((32, 256), F32))
        top = jnp.max(top, axis=0, keepdims=True)
        tsend[k, m] = top
        scale = jnp.where(top > TINY, 1.0 / jnp.maximum(top, TINY), 0.0)

        def code(i, _):
            r = pl.ds(pl.multiple_of(i * 32, 32), 32)
            value = rbuf[k, m, 1 - xl, r]
            share = jnp.abs(value) * scale
            root = share * lax.rsqrt(jnp.maximum(share, TINY))
            level = (root * LEVELS + 0.5).astype(jnp.int32)
            xsend[k, m, r] = jnp.where(value < 0, -level, level).astype(jnp.int16)
            return 0

        lax.fori_loop(0, UNITS // 32, code, 0)
        push(tsend.at[k, m], trecv.at[k, m], partner, top_sem[k][m])
        push(xsend.at[k, m], xrecv.at[k, m], partner, line_sem[k][m])

    base = 1024 - PIECE * e

    def rows_of(t):
        return pl.ds(pl.multiple_of(base + UNITS * t, 32), UNITS)

    part_of = (pl.ds(0, 1), pl.ds(1, 2))
    own_sem, cross_sem, relay_sem = (
        [[[recv.take() for _ in (0, 1)] for _ in (0, 1)] for _ in range(CHUNKS)] for _ in range(3)
    )

    def units(part, k, q, t):
        return vw.at[part_of[part], chunk_pkgs[k][q], rows_of(t)]

    def finish(k, part):
        for m in (GATE, UP) if part == 0 else (BACK,):
            arrived(trecv.at[k, m], top_sem[k][m])
            arrived(xrecv.at[k, m], line_sem[k][m])

        def total(m, r):
            root = xrecv[k, m, r].astype(F32) * (1.0 / LEVELS)
            return rbuf[k, m, xl, r] + root * jnp.abs(root) * trecv[k, m]

        def body(i, _):
            r = pl.ds(pl.multiple_of(i * 32, 32), 32)
            gate, up = total(GATE, r), total(UP, r)
            sig = 1.0 / (1.0 + jnp.exp(-gate))
            activated = gate * sig
            if part == 0:
                values = ((0, activated * up),)
            else:
                back = total(BACK, r)
                values = ((1, back * up * sig * (1.0 + gate * (1.0 - sig))), (2, back * activated))
            wr = pl.ds(pl.multiple_of(base + UNITS * tensor + i * 32, 32), 32)
            for j, value in values:
                value = value.astype(BF)
                for q in (0, 1):
                    p = chunk_pkgs[k][q]
                    v = value[:, 128 * q : 128 * (q + 1)]
                    vw[j, p, wr] = v
                    sb[j, p, r] = (v.astype(F32) * wrow[p]).astype(BF)
            return 0

        lax.fori_loop(0, UNITS // 32, body, 0)
        for q in (0, 1):
            mine = units(part, k, q, tensor)
            push(mine, mine, partner, cross_sem[k][part][q])
            push(mine, mine, sibling, own_sem[k][part][q])

    def relay(k, part):
        for q in (0, 1):
            theirs = units(part, k, q, (1 - xl) * 2 + c)
            arrived(theirs, cross_sem[k][part][q])
            push(theirs, theirs, sibling, relay_sem[k][part][q])

    def slice_complete(k):
        for part in (0, 1):
            for q in (0, 1):
                arrived(units(part, k, q, xl * 2 + 1 - c), own_sem[k][part][q])
                arrived(units(part, k, q, (1 - xl) * 2 + 1 - c), relay_sem[k][part][q])

    first = xl == 0
    n_down = jnp.where(jnp.logical_or(jnp.logical_not(first), e <= 4), e, 0)
    n_up = jnp.where(jnp.logical_or(first, e >= 3), 7 - e, 0)
    n_from_above = jnp.where(jnp.logical_or(e <= 3, jnp.logical_and(jnp.logical_not(first), e <= 6)), e + 1, 0)
    n_from_below = jnp.where(jnp.logical_or(e >= 4, jnp.logical_and(first, e >= 1)), 8 - e, 0)
    down_sem = [(send.take(7), recv.take(7)) for _ in range(CHUNKS)]
    up_sem = [(send.take(7), recv.take(7)) for _ in range(CHUNKS)]
    down_relay = [(send.take(7), recv.take(7)) for _ in range(CHUNKS)]
    up_relay = [(send.take(7), recv.take(7)) for _ in range(CHUNKS)]
    dp_above, dp_below = dp + 1, dp + 31
    my_pkg = [jnp.where(c == 0, *chunk_pkgs[k]) for k in range(CHUNKS)]
    above_yz = ((dp_above // 4) % 4, dp_above % 4)
    below_yz = ((dp_below // 4) % 4, dp_below % 4)

    def win(p, row):
        return vw.at[:, p, pl.ds(pl.multiple_of(row, PIECE), PIECE)]

    def down_copy(k, j):
        s, r = down_sem[k]
        return pltpu.make_async_remote_copy(
            src_ref=win(my_pkg[k], base + PIECE * j),
            dst_ref=win(my_pkg[k], base + 1024 + PIECE * j),
            send_sem=ssem.at[s + j], recv_sem=rsem.at[r + j],
            device_id=below, device_id_type=MESH,
        )

    def up_copy(k, i):
        s, r = up_sem[k]
        return pltpu.make_async_remote_copy(
            src_ref=win(my_pkg[k], base + PIECE * (e + i)),
            dst_ref=win(my_pkg[k], PIECE * i),
            send_sem=ssem.at[s + i], recv_sem=rsem.at[r + i],
            device_id=above, device_id_type=MESH,
        )

    def loop(n, f):
        def body(j, _):
            f(j)
            return 0

        lax.fori_loop(0, n, body, 0)

    def send_neighbours(k):
        loop(n_down, lambda j: down_copy(k, j).start())
        loop(n_up, lambda j: up_copy(k, j).start())

    def from_above(k, q, j):
        p = jnp.where(q == 0, *pkgs_of(k, *above_yz))
        return win(p, base + SLICE + PIECE * j)

    def from_below(k, q, i):
        p = jnp.where(q == 0, *pkgs_of(k, *below_yz))
        return win(p, PIECE * i)

    def pass_on(ref, sems, j):
        return pltpu.make_async_remote_copy(
            src_ref=ref, dst_ref=ref, send_sem=ssem.at[sems[0] + j], recv_sem=rsem.at[sems[1] + j],
            device_id=sibling, device_id_type=MESH,
        )

    def relay_neighbours(k):
        def one_above(j):
            ref = from_above(k, c, j)
            pltpu.make_async_copy(ref, ref, rsem.at[down_sem[k][1] + j]).wait()
            pass_on(ref, down_relay[k], j).start()

        def one_below(i):
            ref = from_below(k, c, i)
            pltpu.make_async_copy(ref, ref, rsem.at[up_sem[k][1] + i]).wait()
            pass_on(ref, up_relay[k], i).start()

        loop(n_from_above, one_above)
        loop(n_from_below, one_below)

    def neighbours_complete(k):
        def one_above(j):
            ref = from_above(k, 1 - c, j)
            pltpu.make_async_copy(ref, ref, rsem.at[down_relay[k][1] + j]).wait()

        def one_below(i):
            ref = from_below(k, 1 - c, i)
            pltpu.make_async_copy(ref, ref, rsem.at[up_relay[k][1] + i]).wait()

        loop(n_from_above, one_above)
        loop(n_from_below, one_below)

    def neighbours_sent(k):
        loop(n_down, lambda j: down_copy(k, j).wait_send())
        loop(n_up, lambda j: up_copy(k, j).wait_send())
        loop(n_from_above, lambda j: pass_on(from_above(k, c, j), down_relay[k], j).wait_send())
        loop(n_from_below, lambda i: pass_on(from_below(k, c, i), up_relay[k], i).wait_send())

    col_sem = [recv.take() for _ in (0, 1)]
    col_send = [send.take(2) for _ in (0, 1)]
    col_here = [here.take() for _ in (0, 1)]
    holder = c == y // 2
    at_home = xl == xh
    col_start = pl.multiple_of(e * 256, 256)

    def col_copies(a):
        src = xt.at[a, :, :, pl.ds(col_start, 256)]
        make = lambda to, i: pltpu.make_async_remote_copy(
            src_ref=src, dst_ref=cols.at[a], send_sem=ssem.at[col_send[a] + i], recv_sem=rsem.at[col_sem[a]],
            device_id=to, device_id_type=MESH,
        )
        return make(sibling, 0), make(across[0], 0), make(across[1], 1), pltpu.make_async_copy(
            src, cols.at[a], lsem.at[col_here[a]]
        )

    home_holder = jnp.logical_and(holder, at_home)
    far_holder = jnp.logical_and(holder, jnp.logical_not(at_home))

    def send_cols(a):
        home, far0, far1, local = col_copies(a)

        @pl.when(home_holder)
        def _():
            home.start()
            local.start()

        @pl.when(far_holder)
        def _():
            far0.start()
            far1.start()

    def cols_complete(a):
        _, _, _, local = col_copies(a)

        @pl.when(home_holder)
        def _():
            local.wait()

        @pl.when(jnp.logical_not(home_holder))
        def _():
            arrived(cols.at[a], col_sem[a])

    def cols_sent(a):
        home, far0, far1, _ = col_copies(a)

        @pl.when(home_holder)
        def _():
            home.wait_send()

        @pl.when(far_holder)
        def _():
            far0.wait_send()
            far1.wait_send()

    cov_out = (act_o, grad_o)

    def full_cov(a):
        rhs = cols[a].reshape(1024, 256)

        def body(i, _):
            k = pl.ds(pl.multiple_of(i * 256, 256), 256)
            parts = [
                (xt[a, p, :, k].astype(F32) * wcol[:, p : p + 1]).astype(BF) for p in range(8)
            ]
            cov_out[a][k] = lax.dot_general(
                jnp.concatenate(parts, axis=0), rhs, (((0,), (0,)), ((), ())), preferred_element_type=F32
            )
            return 0

        lax.fori_loop(0, 8, body, 0)

    split_row = PIECE * e - UNITS * tensor
    blk_out = (hid_o, gg_o, ug_o)

    def block_cov(j):
        def body(i, _):
            k = pl.multiple_of(i * 256, 256)
            lhs = jnp.concatenate([sb[j, p] for p in range(8)], axis=1)

            def product(start):
                rhs = jnp.concatenate([vw[j, p, pl.ds(start + k, 256)] for p in range(8)], axis=1)
                return lax.dot_general(lhs, rhs, (((1,), (1,)), ((), ())), preferred_element_type=F32)

            @pl.when(split_row < UNITS)
            def _():
                blk_out[j][:, pl.ds(k, 256)] = product(1024)

            @pl.when(split_row > 0)
            def _():
                row = lax.broadcasted_iota(jnp.int32, (UNITS, 256), 0)
                blk_out[j][:, pl.ds(k, 256)] = jnp.where(
                    row < split_row, product(0), blk_out[j][:, pl.ds(k, 256)]
                )

            return 0

        lax.fori_loop(0, 4, body, 0)

    def pocket_weights():
        ids = ids_ref[...]
        weights = jnp.zeros((8, 128), F32)
        for k in range(POCKETS):
            member = (ids == k).astype(F32)
            count = jnp.sum(jnp.sum(member, axis=1, keepdims=True), axis=0, keepdims=True)
            weights = weights + member * (1.0 / (POCKETS * count))
        for p in range(8):
            wrow[p] = weights[p : p + 1]
        wcol[...] = weights.T

    start_twin(0)
    start_twin(1)
    start_ring(0)
    pocket_weights()
    forward_twin(0)
    start_ring(1)
    forward_twin(1)
    send_packages(0)
    project(0, GATE)
    project(0, UP)
    combine(0, GATE)
    send_packages(1)
    project(0, BACK)
    combine(0, UP)
    combine(0, BACK)
    finish(0, 0)
    forward_packages(0)
    project(1, GATE)
    project(1, UP)
    combine(1, GATE)
    project(2, GATE)
    combine(1, UP)
    project(2, UP)
    combine(2, GATE)
    combine(2, UP)
    finish(0, 1)
    forward_packages(1)
    project(1, BACK)
    project(2, BACK)
    combine(1, BACK)
    combine(2, BACK)
    finish(1, 0)
    finish(2, 0)
    relay(0, 0)
    relay(0, 1)
    far_packages(0)
    send_cols(0)
    project(3, GATE)
    project(3, UP)
    combine(3, GATE)
    combine(3, UP)
    slice_complete(0)
    send_neighbours(0)
    finish(1, 1)
    finish(2, 1)
    far_packages(1)
    send_cols(1)
    project(3, BACK)
    combine(3, BACK)
    finish(3, 0)
    for k in (1, 2):
        relay(k, 0)
    for k in (1, 2):
        relay(k, 1)
        slice_complete(k)
        send_neighbours(k)
    relay_neighbours(0)
    finish(3, 1)
    cols_complete(0)
    full_cov(0)
    relay(3, 0)
    relay(3, 1)
    slice_complete(3)
    send_neighbours(3)
    relay_neighbours(1)
    cols_complete(1)
    full_cov(1)
    relay_neighbours(2)
    relay_neighbours(3)
    for k in range(CHUNKS):
        neighbours_complete(k)
    for j in range(3):
        block_cov(j)
    for wait in slot_sent + unsent:
        wait()
    for k in range(CHUNKS):
        neighbours_sent(k)
    for a in (0, 1):
        cols_sent(a)


N_SEND, N_RECV, N_LOCAL = 380, 320, 24


def local(tokens, out_grad, gate_weight, up_weight, down_weight, pocket_ids):
    ids = pocket_ids.reshape(2, 4, 4, 2, 16)
    ids = jnp.concatenate(
        [
            ids[:, :, :, 0].transpose(1, 0, 2, 3).reshape(4, 128),
            ids[:, :, :, 1].transpose(2, 0, 1, 3).reshape(4, 128),
        ]
    )
    any_spec = pl.BlockSpec(memory_space=pl.ANY)
    vmem = pl.BlockSpec(memory_space=pltpu.VMEM)
    return pl.pallas_call(
        kernel,
        out_shape=[
            pltpu.VMEM((2048, 256), F32),
            pltpu.VMEM((2048, 256), F32),
            pltpu.VMEM((UNITS, 1024), F32),
            pltpu.VMEM((UNITS, 1024), F32),
            pltpu.VMEM((UNITS, 1024), F32),
        ],
        in_specs=[any_spec] * 5 + [vmem],
        out_specs=[vmem] * 5,
        scratch_shapes=[
            pltpu.VMEM((2, 8, 128, 2048), BF),
            pltpu.VMEM((2048, SLICE), BF),
            pltpu.VMEM((2048, SLICE), BF),
            pltpu.VMEM((SLICE, 2048), BF),
            pltpu.VMEM((3, 2, 2, UNITS, 256), F32),
            pltpu.VMEM((CHUNKS, 3, 2, UNITS, 256), F32),
            pltpu.VMEM((CHUNKS, 3, UNITS, 256), jnp.int16),
            pltpu.VMEM((CHUNKS, 3, UNITS, 256), jnp.int16),
            pltpu.VMEM((CHUNKS, 3, 1, 256), F32),
            pltpu.VMEM((CHUNKS, 3, 1, 256), F32),
            pltpu.VMEM((3, 8, 2048, 128), BF),
            pltpu.VMEM((3, 8, UNITS, 128), BF),
            pltpu.VMEM((2, 8, 128, 256), BF),
            pltpu.VMEM((8, 1, 128), F32),
            pltpu.VMEM((128, 8), F32),
            pltpu.SemaphoreType.DMA((N_SEND,)),
            pltpu.SemaphoreType.DMA((N_RECV,)),
            pltpu.SemaphoreType.DMA((N_LOCAL,)),
        ],
        compiler_params=pltpu.CompilerParams(
            collective_id=0, has_side_effects=True, vmem_limit_bytes=52 * MIB
        ),
        name="ekfac_factors",
    )(tokens, out_grad, gate_weight, up_weight, down_weight, ids)


def solution(mesh):
    return jax.shard_map(
        local,
        mesh=mesh,
        in_specs=(
            P("dp", "tensor"),
            P("dp", "tensor"),
            P("tensor", "dp"),
            P("tensor", "dp"),
            P("dp", "tensor"),
            P(),
        ),
        out_specs=(
            P("tensor", "dp"),
            P("tensor", "dp"),
            P(("dp", "tensor"), None),
            P(("dp", "tensor"), None),
            P(("dp", "tensor"), None),
        ),
        check_vma=False,
    )
```

```python
import functools

import jax
import jax.numpy as jnp
from jax import lax
from jax.experimental import pallas as pl
from jax.experimental.pallas import tpu as pltpu
from jax.sharding import PartitionSpec as P

MESH = pl.DeviceIdType.MESH
POCKETS = 16
BF = jnp.bfloat16
F32 = jnp.float32
MIB = 1 << 20
CHUNKS = 4
UNITS = 224
SLICE = 896
PIECE = 128
GATE, UP, BACK = 0, 1, 2
LEVELS = 32767.0
TINY = 1e-30


def mod4(v):
    return lax.rem(v + 4, 4)


class Sems:
    def __init__(self, ref):
        self.ref, self.used = ref, 0

    def take(self, count=1):
        base = self.used
        self.used += count
        return base


def kernel(
    tok, grd, gate_h, up_h, down_h, ids_ref,
    act_o, grad_o, hid_o, gg_o, ug_o,
    xt, wg, wu, wd, pbuf, rbuf, xsend, xrecv, tsend, trecv, vw, sb, cols, stage, res, wrow, wcol,
    ssem, rsem, lsem,
):
    dp = lax.axis_index("dp")
    tensor = lax.axis_index("tensor")
    xh, y, z = dp // 16, (dp // 4) % 4, dp % 4
    xl, c = tensor // 2, tensor % 2
    e = dp % 8

    def dev(xh_, y_, z_, xl_, c_):
        return {"dp": xh_ * 16 + y_ * 4 + z_, "tensor": xl_ * 2 + c_}

    sibling = dev(xh, y, z, xl, 1 - c)
    partner = dev(xh, y, z, 1 - xl, c)
    twin = dev(1 - xh, y, z, xl, c)
    y_peer = [dev(xh, mod4(y + s), z, xl, c) for s in (1, 2, 3)]
    z_peer = [dev(xh, y, mod4(z + s), xl, c) for s in (1, 2, 3)]
    around = [{"dp": lax.rem(dp + s, 32), "tensor": t} for s in (1, 31) for t in range(4)]
    above, below = ({"dp": lax.rem(dp + s, 32), "tensor": tensor} for s in (1, 31))
    across = [dev(1 - xh, y, z, 1 - xl, k) for k in (0, 1)]

    send, recv, here = Sems(ssem), Sems(rsem), Sems(lsem)
    groups = {}

    def push(src, dst, to, r, group):
        s = groups.setdefault(group, None)
        if s is None:
            s = groups[group] = send.take()
        copy = pltpu.make_async_remote_copy(
            src_ref=src, dst_ref=dst, send_sem=ssem.at[s], recv_sem=rsem.at[r],
            device_id=to, device_id_type=MESH,
        )
        copy.start()
        return copy

    def group_sent(group, ref):
        pltpu.make_async_copy(ref, ref, ssem.at[groups.pop(group)]).wait()

    def arrived(ref, r):
        pltpu.make_async_copy(ref, ref, rsem.at[r]).wait()

    def stay(src, dst):
        copy = pltpu.make_async_copy(src, dst, lsem.at[here.take()])
        copy.start()
        return copy

    shard = (tok, grd)
    pkg_of = (y, 4 + z)
    inner = (xh * 64 + z * 16, xh * 64 + y * 16)
    twin_inner = ((1 - xh) * 64 + z * 16, (1 - xh) * 64 + y * 16)

    def rows16(ref, a, half, start):
        return ref.at[a, pkg_of[half], pl.ds(pl.multiple_of(start, 16), 16)]

    own_copies = [
        [stay(shard[a].at[pl.ds(16 * h, 16)], rows16(xt, a, h, inner[h])) for h in (0, 1)]
        for a in (0, 1)
    ]
    weight_copies = [stay(gate_h, wg), stay(up_h, wu), stay(down_h, wd)]

    def pocket_weights():
        ids = ids_ref[...]
        weights = jnp.zeros((8, 128), F32)
        for k in range(POCKETS):
            member = (ids == k).astype(F32)
            count = jnp.sum(jnp.sum(member, axis=1, keepdims=True), axis=0, keepdims=True)
            weights = weights + member * (1.0 / (POCKETS * count))
        for p in range(8):
            wrow[p] = weights[p : p + 1]
        wcol[...] = weights.T

    pocket_weights()

    barrier = pltpu.get_barrier_semaphore()
    greeted = [sibling, partner, twin, *y_peer, *z_peer, *across, *around]
    for peer in greeted:
        pl.semaphore_signal(barrier, inc=1, device_id=peer, device_id_type=MESH)
    pl.semaphore_wait(barrier, len(greeted))

    twin_sem = [[recv.take() for _ in (0, 1)] for _ in (0, 1)]
    ring_sem = [[recv.take() for _ in (0, 1)] for _ in (0, 1)]
    ring_peer = (z_peer, y_peer)
    def start_twin(a):
        for h in (0, 1):
            push(shard[a].at[pl.ds(16 * h, 16)], rows16(xt, a, h, inner[h]), twin, twin_sem[a][h], "twin")

    def start_ring(a):
        for h in (0, 1):
            for peer in ring_peer[h]:
                push(shard[a].at[pl.ds(16 * h, 16)], rows16(xt, a, h, inner[h]), peer, ring_sem[a][h], "ring")

    def forward_twin(a):
        for h in (0, 1):
            piece = rows16(xt, a, h, twin_inner[h])
            arrived(piece, twin_sem[a][h])
            for peer in ring_peer[h]:
                push(piece, piece, peer, ring_sem[a][h], "ring")

    side_peer = ((y_peer[2], y_peer[0]), (z_peer[2], z_peer[0]))
    side_sem = [[[recv.take() for _ in (0, 1)] for _ in (0, 1)] for _ in (0, 1)]
    far_sem = [[[recv.take() for _ in (0, 1)] for _ in (0, 1)] for _ in (0, 1)]
    coord = (y, z)

    def package(h, step):
        return 4 * h + mod4(coord[h] + step)

    def send_packages(a):
        for h in (0, 1):
            own_copies[a][h].wait()
            arrived(xt.at[a, pkg_of[h], pl.ds(0, 96)], ring_sem[a][h])
            whole = xt.at[a, pkg_of[h]]
            for s in (0, 1):
                push(whole, whole, side_peer[h][s], side_sem[a][h][1 - s], "side")

    def forward_packages(a):
        for h in (0, 1):
            for s in (0, 1):
                whole = xt.at[a, package(h, (-1, 1)[s])]
                arrived(whole, side_sem[a][h][s])
                part = xt.at[a, package(h, (-1, 1)[s]), pl.ds(64 * s, 64)]
                push(part, part, side_peer[h][1 - s], far_sem[a][h][s], "far")

    def far_packages(a):
        for h in (0, 1):
            for s in (0, 1):
                arrived(xt.at[a, package(h, 2), pl.ds(64 * s, 64)], far_sem[a][h][s])

    chunk_pkgs = [
        (package(0, 0), package(1, 0)),
        (package(0, -1), package(0, 1)),
        (package(1, -1), package(1, 1)),
        (package(0, 2), package(1, 2)),
    ]

    def pkgs_of(k, y_, z_):
        return [
            (y_, 4 + z_),
            (mod4(y_ - 1), mod4(y_ + 1)),
            (4 + mod4(z_ - 1), 4 + mod4(z_ + 1)),
            (mod4(y_ + 2), 4 + mod4(z_ + 2)),
        ][k]

    core_sem = [[recv.take() for _ in range(3)] for _ in range(CHUNKS)]
    line_sem = [[recv.take() for _ in range(3)] for _ in range(CHUNKS)]
    top_sem = [[recv.take() for _ in range(3)] for _ in range(CHUNKS)]
    slot_of = {}
    slot_sent = [None] * 3
    weights_in = [False] * 3

    def project(k, m):
        if not weights_in[m]:
            weight_copies[m].wait()
            weights_in[m] = True
        slot = len(slot_of) % 3
        assert slot not in busy.values()
        a = 1 if m == BACK else 0
        x = jnp.concatenate([xt[a, chunk_pkgs[k][0]], xt[a, chunk_pkgs[k][1]]], axis=0)
        if m == BACK:
            part = lax.dot_general(wd[...], x, (((1,), (1,)), ((), ())), preferred_element_type=F32)
        else:
            w = (wg, wu)[m]
            part = lax.dot_general(w[...], x, (((0,), (1,)), ((), ())), preferred_element_type=F32)
        if slot_sent[slot] is not None:
            slot_sent[slot].wait_send()
        for i in range(4):
            pbuf[slot, i // 2, i % 2] = part[UNITS * i : UNITS * (i + 1)]
        slot_sent[slot] = push(pbuf.at[slot, :, 1 - c], rbuf.at[k, m], sibling, core_sem[k][m], slot)
        slot_of[k, m] = slot
        busy[k, m] = slot

    busy = {}

    def combine(k, m):
        slot = busy.pop((k, m))
        arrived(rbuf.at[k, m], core_sem[k][m])

        def add(i, top):
            r = pl.ds(pl.multiple_of(i * 32, 32), 32)
            value = rbuf[k, m, 1 - xl, r] + pbuf[slot, 1 - xl, c, r]
            rbuf[k, m, 1 - xl, r] = value
            rbuf[k, m, xl, r] = rbuf[k, m, xl, r] + pbuf[slot, xl, c, r]
            return jnp.maximum(top, jnp.abs(value))

        top = lax.fori_loop(0, UNITS // 32, add, jnp.zeros((32, 256), F32))
        top = jnp.max(top, axis=0, keepdims=True)
        tsend[k, m] = top
        scale = jnp.where(top > TINY, 1.0 / jnp.maximum(top, TINY), 0.0)

        def code(i, _):
            r = pl.ds(pl.multiple_of(i * 32, 32), 32)
            value = rbuf[k, m, 1 - xl, r]
            share = jnp.abs(value) * scale
            root = share * lax.rsqrt(jnp.maximum(share, TINY))
            level = (root * LEVELS + 0.5).astype(jnp.int32)
            xsend[k, m, r] = jnp.where(value < 0, -level, level).astype(jnp.int16)
            return 0

        lax.fori_loop(0, UNITS // 32, code, 0)
        push(tsend.at[k, m], trecv.at[k, m], partner, top_sem[k][m], "top")
        push(xsend.at[k, m], xrecv.at[k, m], partner, line_sem[k][m], "line")

    base = 1024 - PIECE * e

    def rows_of(t):
        return pl.ds(pl.multiple_of(base + UNITS * t, 32), UNITS)

    part_of = (pl.ds(0, 1), pl.ds(1, 2))
    own_sem, cross_sem, relay_sem = (
        [[recv.take() for _ in (0, 1)] for _ in range(CHUNKS)] for _ in range(3)
    )

    def units(part, k, q, t):
        return vw.at[part_of[part], chunk_pkgs[k][q], rows_of(t)]

    def units_arrived(part, t, r):
        arrived(vw.at[part_of[part], pl.ds(0, 2), rows_of(t)], r)

    def finish(k, part):
        for m in (GATE, UP) if part == 0 else (BACK,):
            arrived(trecv.at[k, m], top_sem[k][m])
            arrived(xrecv.at[k, m], line_sem[k][m])

        def total(m, r):
            root = xrecv[k, m, r].astype(F32) * (1.0 / LEVELS)
            return rbuf[k, m, xl, r] + root * jnp.abs(root) * trecv[k, m]

        def body(i, _):
            r = pl.ds(pl.multiple_of(i * 32, 32), 32)
            gate, up = total(GATE, r), total(UP, r)
            sig = 1.0 / (1.0 + jnp.exp(-gate))
            activated = gate * sig
            if part == 0:
                values = ((0, activated * up),)
            else:
                back = total(BACK, r)
                values = ((1, back * up * sig * (1.0 + gate * (1.0 - sig))), (2, back * activated))
            wr = pl.ds(pl.multiple_of(base + UNITS * tensor + i * 32, 32), 32)
            for j, value in values:
                value = value.astype(BF)
                for q in (0, 1):
                    p = chunk_pkgs[k][q]
                    v = value[:, 128 * q : 128 * (q + 1)]
                    vw[j, p, wr] = v
                    sb[j, p, r] = (v.astype(F32) * wrow[p]).astype(BF)
            return 0

        lax.fori_loop(0, UNITS // 32, body, 0)
        for q in (0, 1):
            mine = units(part, k, q, tensor)
            push(mine, mine, partner, cross_sem[k][part], "cross")
        for q in (0, 1):
            mine = units(part, k, q, tensor)
            push(mine, mine, sibling, own_sem[k][part], "own")

    def relay(k, part):
        units_arrived(part, (1 - xl) * 2 + c, cross_sem[k][part])
        for q in (0, 1):
            theirs = units(part, k, q, (1 - xl) * 2 + c)
            push(theirs, theirs, sibling, relay_sem[k][part], "relay")

    def slice_complete(k):
        for part in (0, 1):
            units_arrived(part, xl * 2 + 1 - c, own_sem[k][part])
            units_arrived(part, (1 - xl) * 2 + 1 - c, relay_sem[k][part])

    low = e <= 3
    n_down = jnp.where(e <= 4, e, 0)
    n_up = jnp.where(jnp.logical_and(e >= 3, e <= 6), 7 - e, 0)
    n_near = jnp.where(low, e + 1, 8 - e)
    near_row = jnp.where(low, base + SLICE, 0)
    near_dp = jnp.where(low, dp + 1, dp + 31)
    near_y, near_z = (near_dp // 4) % 4, near_dp % 4
    my_pkg = [jnp.where(c == 0, *chunk_pkgs[k]) for k in range(CHUNKS)]
    near_pkg = [jnp.where(c == 0, *pkgs_of(k, near_y, near_z)) for k in range(CHUNKS)]
    near_sem, near_relay = ([recv.take() for _ in range(CHUNKS)] for _ in range(2))
    down_send, up_send, near_send = ([send.take() for _ in range(CHUNKS)] for _ in range(3))

    def sized(count, most, f):
        for n in range(1, most + 1):
            pl.when(count == n)(functools.partial(f, n))

    def win(p, row, n):
        return vw.at[:, p, pl.ds(pl.multiple_of(row, PIECE), n * PIECE)]

    def down_copy(k, n):
        return pltpu.make_async_remote_copy(
            src_ref=win(my_pkg[k], base, n), dst_ref=win(my_pkg[k], base + 1024, n),
            send_sem=ssem.at[down_send[k]], recv_sem=rsem.at[near_sem[k]],
            device_id=below, device_id_type=MESH,
        )

    def up_copy(k, n):
        return pltpu.make_async_remote_copy(
            src_ref=win(my_pkg[k], base + PIECE * e, n), dst_ref=win(my_pkg[k], 0, n),
            send_sem=ssem.at[up_send[k]], recv_sem=rsem.at[near_sem[k]],
            device_id=above, device_id_type=MESH,
        )

    def near_copy(k, n):
        ref = win(near_pkg[k], near_row, n)
        return pltpu.make_async_remote_copy(
            src_ref=ref, dst_ref=ref, send_sem=ssem.at[near_send[k]], recv_sem=rsem.at[near_relay[k]],
            device_id=sibling, device_id_type=MESH,
        )

    def send_neighbours(k):
        sized(n_down, 4, lambda n: down_copy(k, n).start())
        sized(n_up, 4, lambda n: up_copy(k, n).start())

    def relay_neighbours(k):
        def go(n):
            arrived(win(near_pkg[k], near_row, n), near_sem[k])
            near_copy(k, n).start()

        sized(n_near, 4, go)

    def neighbours_complete(k):
        sized(n_near, 4, lambda n: arrived(win(near_pkg[k], near_row, n), near_relay[k]))

    def neighbours_sent(k):
        sized(n_down, 4, lambda n: down_copy(k, n).wait_send())
        sized(n_up, 4, lambda n: up_copy(k, n).wait_send())
        sized(n_near, 4, lambda n: near_copy(k, n).wait_send())

    major = jnp.logical_or(e <= 2, e >= 5)
    n_cols = jnp.where(low, 7 - e, e)
    first_col = jnp.where(low, e, 0)
    res_sem = recv.take(8)
    res_send = send.take(24)
    pair = (tensor, tensor + 4)

    def result_copy(i, r, h):
        row = jnp.where(low, 0, PIECE * (e - 1)) + PIECE * i + 32 * r
        owner = row // UNITS
        col = jnp.where(low, 0, 8 - e) + pair[h]
        return pltpu.make_async_remote_copy(
            src_ref=stage.at[:, i, pl.ds(32 * r, 32), pl.ds(128 * h, 128)],
            dst_ref=res.at[
                :, pl.ds(pl.multiple_of(row - UNITS * owner, 32), 32), pl.ds(pl.multiple_of(128 * col, 128), 128)
            ],
            send_sem=ssem.at[res_send + 8 * i + 2 * r + h], recv_sem=rsem.at[res_sem + col],
            device_id={"dp": near_dp % 32, "tensor": owner}, device_id_type=MESH,
        )

    def each_result(i, f):
        for h in (0, 1):
            @pl.when(pair[h] < n_cols)
            def _():
                for r in range(4):
                    f(result_copy(i, r, h))

    def products_for_neighbour():
        def body(i, _):
            rows = pl.ds(pl.multiple_of(near_row + PIECE * i, PIECE), PIECE)
            cols_at = [
                pl.ds(pl.multiple_of(base + PIECE * (first_col + jnp.minimum(piece, n_cols - 1)), PIECE), PIECE)
                for piece in pair
            ]
            for j in range(3):
                lhs = jnp.concatenate(
                    [(vw[j, p, rows].astype(F32) * wrow[p]).astype(BF) for p in range(8)], axis=1
                )
                rhs = jnp.concatenate(
                    [jnp.concatenate([vw[j, p, at] for at in cols_at], axis=0) for p in range(8)], axis=1
                )
                stage[j, i] = lax.dot_general(
                    lhs, rhs, (((1,), (1,)), ((), ())), preferred_element_type=F32
                ).astype(BF)
            each_result(i, lambda copy: copy.start())
            return 0

        @pl.when(major)
        def _():
            lax.fori_loop(0, n_near, body, 0)

    def products_sent():
        def body(i, _):
            each_result(i, lambda copy: copy.wait_send())
            return 0

        @pl.when(major)
        def _():
            lax.fori_loop(0, n_near, body, 0)

    col_sem = [recv.take() for _ in (0, 1)]
    col_send = [send.take(2) for _ in (0, 1)]
    col_here = [here.take() for _ in (0, 1)]
    holder = c == y // 2
    at_home = xl == xh
    col_start = pl.multiple_of(e * 256, 256)

    def col_copies(a):
        src = xt.at[a, :, :, pl.ds(col_start, 256)]
        make = lambda to, i: pltpu.make_async_remote_copy(
            src_ref=src, dst_ref=cols.at[a], send_sem=ssem.at[col_send[a] + i], recv_sem=rsem.at[col_sem[a]],
            device_id=to, device_id_type=MESH,
        )
        return make(sibling, 0), make(across[0], 0), make(across[1], 1), pltpu.make_async_copy(
            src, cols.at[a], lsem.at[col_here[a]]
        )

    home_holder = jnp.logical_and(holder, at_home)
    far_holder = jnp.logical_and(holder, jnp.logical_not(at_home))

    def send_cols(a):
        home, far0, far1, local = col_copies(a)

        @pl.when(home_holder)
        def _():
            home.start()
            local.start()

        @pl.when(far_holder)
        def _():
            far0.start()
            far1.start()

    def cols_complete(a):
        _, _, _, local = col_copies(a)

        @pl.when(home_holder)
        def _():
            local.wait()

        @pl.when(jnp.logical_not(home_holder))
        def _():
            arrived(cols.at[a], col_sem[a])

    def cols_sent(a):
        home, far0, far1, _ = col_copies(a)

        @pl.when(home_holder)
        def _():
            home.wait_send()

        @pl.when(far_holder)
        def _():
            far0.wait_send()
            far1.wait_send()

    cov_out = (act_o, grad_o)

    def full_cov(a):
        rhs = cols[a].reshape(1024, 256)

        def body(i, _):
            k = pl.ds(pl.multiple_of(i * 256, 256), 256)
            parts = [
                (xt[a, p, :, k].astype(F32) * wcol[:, p : p + 1]).astype(BF) for p in range(8)
            ]
            cov_out[a][k] = lax.dot_general(
                jnp.concatenate(parts, axis=0), rhs, (((0,), (0,)), ((), ())), preferred_element_type=F32
            )
            return 0

        lax.fori_loop(0, 8, body, 0)

    split_row = jnp.clip(PIECE * e - UNITS * tensor, 0, UNITS)
    has_early, has_late = split_row > 0, split_row < UNITS
    blk_out = (hid_o, gg_o, ug_o)

    def block_cov():
        row = lax.broadcasted_iota(jnp.int32, (UNITS, 256), 0)

        def body(g, _):
            k = pl.multiple_of(g * 256, 256)

            def product(j, start):
                lhs = jnp.concatenate([sb[j, p] for p in range(8)], axis=1)
                rhs = jnp.concatenate([vw[j, p, pl.ds(start + k, 256)] for p in range(8)], axis=1)
                return lax.dot_general(lhs, rhs, (((1,), (1,)), ((), ())), preferred_element_type=F32)

            @pl.when(jnp.logical_and(has_late, jnp.logical_or(low, 2 * g <= 6 - e)))
            def _():
                for j in range(3):
                    blk_out[j][:, pl.ds(k, 256)] = product(j, 1024)

            @pl.when(jnp.logical_and(has_early, jnp.logical_or(jnp.logical_not(low), 2 * g + 1 >= 8 - e)))
            def _():
                for j in range(3):
                    blk_out[j][:, pl.ds(k, 256)] = jnp.where(
                        row < split_row, product(j, 0), blk_out[j][:, pl.ds(k, 256)]
                    )

            return 0

        lax.fori_loop(0, 4, body, 0)

    def products_from_neighbour():
        row = lax.broadcasted_iota(jnp.int32, (UNITS, 128), 0)
        minor_early = jnp.logical_and(jnp.logical_and(low, e >= 1), has_early)
        minor_late = jnp.logical_and(jnp.logical_and(jnp.logical_not(low), e <= 6), has_late)
        bands = jnp.where(low, split_row, UNITS - split_row) // 32
        start = jnp.where(low, 0, 7 - e)
        stop = jnp.where(low, 8 - e, 8)
        from_row = jnp.where(low, 0, split_row)
        to_row = jnp.where(low, split_row, UNITS)

        def body(col, _):
            sized(bands, 7, lambda n: arrived(res.at[:, pl.ds(0, 32 * n), pl.ds(0, 128)], res_sem + col))
            at = pl.ds(pl.multiple_of(col * 128, 128), 128)
            here_too = jnp.logical_and(row >= from_row, row < to_row)
            for j in range(3):
                blk_out[j][:, at] = jnp.where(here_too, res[j, :, at].astype(F32), blk_out[j][:, at])
            return 0

        @pl.when(jnp.logical_or(minor_early, minor_late))
        def _():
            lax.fori_loop(start, stop, body, 0)

    start_twin(0)
    start_ring(0)
    start_twin(1)
    forward_twin(0)
    start_ring(1)
    forward_twin(1)
    send_packages(0)
    project(0, GATE)
    project(0, UP)
    combine(0, GATE)
    send_packages(1)
    project(0, BACK)
    combine(0, UP)
    combine(0, BACK)
    finish(0, 0)
    forward_packages(0)
    project(1, GATE)
    project(1, UP)
    combine(1, GATE)
    project(2, GATE)
    combine(1, UP)
    project(2, UP)
    combine(2, GATE)
    combine(2, UP)
    finish(0, 1)
    forward_packages(1)
    project(1, BACK)
    project(2, BACK)
    combine(1, BACK)
    combine(2, BACK)
    finish(1, 0)
    finish(2, 0)
    relay(0, 0)
    relay(0, 1)
    far_packages(0)
    send_cols(0)
    project(3, GATE)
    project(3, UP)
    combine(3, GATE)
    combine(3, UP)
    slice_complete(0)
    send_neighbours(0)
    finish(1, 1)
    finish(2, 1)
    far_packages(1)
    send_cols(1)
    project(3, BACK)
    combine(3, BACK)
    finish(3, 0)
    for k in (1, 2):
        relay(k, 0)
    for k in (1, 2):
        relay(k, 1)
        slice_complete(k)
        send_neighbours(k)
    relay_neighbours(0)
    finish(3, 1)
    cols_complete(0)
    full_cov(0)
    relay(3, 0)
    relay(3, 1)
    slice_complete(3)
    send_neighbours(3)
    relay_neighbours(1)
    cols_complete(1)
    full_cov(1)
    relay_neighbours(2)
    relay_neighbours(3)
    for k in range(CHUNKS):
        neighbours_complete(k)
    products_for_neighbour()
    block_cov()
    products_from_neighbour()
    for copy in slot_sent:
        copy.wait_send()
    group_sent("twin", xt.at[0, 0, pl.ds(0, 64)])
    group_sent("ring", xt.at[0, pl.ds(0, 3)])
    group_sent("side", xt.at[0])
    group_sent("far", xt.at[0, pl.ds(0, 4)])
    group_sent("top", tsend)
    group_sent("line", xsend)
    group_sent("cross", sb)
    group_sent("own", sb)
    group_sent("relay", sb)
    for k in range(CHUNKS):
        neighbours_sent(k)
    for a in (0, 1):
        cols_sent(a)
    products_sent()
    assert (send.used, recv.used, here.used) == (N_SEND, N_RECV, N_LOCAL)


N_SEND, N_RECV, N_LOCAL = 52, 102, 9


def local(tokens, out_grad, gate_weight, up_weight, down_weight, pocket_ids):
    ids = pocket_ids.reshape(2, 4, 4, 2, 16)
    ids = jnp.concatenate(
        [
            ids[:, :, :, 0].transpose(1, 0, 2, 3).reshape(4, 128),
            ids[:, :, :, 1].transpose(2, 0, 1, 3).reshape(4, 128),
        ]
    )
    any_spec = pl.BlockSpec(memory_space=pl.ANY)
    vmem = pl.BlockSpec(memory_space=pltpu.VMEM)
    return pl.pallas_call(
        kernel,
        out_shape=[
            pltpu.VMEM((2048, 256), F32),
            pltpu.VMEM((2048, 256), F32),
            pltpu.VMEM((UNITS, 1024), F32),
            pltpu.VMEM((UNITS, 1024), F32),
            pltpu.VMEM((UNITS, 1024), F32),
        ],
        in_specs=[any_spec] * 5 + [vmem],
        out_specs=[vmem] * 5,
        scratch_shapes=[
            pltpu.VMEM((2, 8, 128, 2048), BF),
            pltpu.VMEM((2048, SLICE), BF),
            pltpu.VMEM((2048, SLICE), BF),
            pltpu.VMEM((SLICE, 2048), BF),
            pltpu.VMEM((3, 2, 2, UNITS, 256), F32),
            pltpu.VMEM((CHUNKS, 3, 2, UNITS, 256), F32),
            pltpu.VMEM((CHUNKS, 3, UNITS, 256), jnp.int16),
            pltpu.VMEM((CHUNKS, 3, UNITS, 256), jnp.int16),
            pltpu.VMEM((CHUNKS, 3, 1, 256), F32),
            pltpu.VMEM((CHUNKS, 3, 1, 256), F32),
            pltpu.VMEM((3, 8, 2048, 128), BF),
            pltpu.VMEM((3, 8, UNITS, 128), BF),
            pltpu.VMEM((2, 8, 128, 256), BF),
            pltpu.VMEM((3, 3, 128, 256), BF),
            pltpu.VMEM((3, UNITS, 1024), BF),
            pltpu.VMEM((8, 1, 128), F32),
            pltpu.VMEM((128, 8), F32),
            pltpu.SemaphoreType.DMA((N_SEND,)),
            pltpu.SemaphoreType.DMA((N_RECV,)),
            pltpu.SemaphoreType.DMA((N_LOCAL,)),
        ],
        compiler_params=pltpu.CompilerParams(
            collective_id=0, has_side_effects=True, vmem_limit_bytes=52 * MIB
        ),
        name="ekfac_factors",
    )(tokens, out_grad, gate_weight, up_weight, down_weight, ids)


def solution(mesh):
    return jax.shard_map(
        local,
        mesh=mesh,
        in_specs=(
            P("dp", "tensor"),
            P("dp", "tensor"),
            P("tensor", "dp"),
            P("tensor", "dp"),
            P("dp", "tensor"),
            P(),
        ),
        out_specs=(
            P("tensor", "dp"),
            P("tensor", "dp"),
            P(("dp", "tensor"), None),
            P(("dp", "tensor"), None),
            P(("dp", "tensor"), None),
        ),
        check_vma=False,
    )
```

```python
import functools

import jax
import jax.numpy as jnp
from jax import lax
from jax.experimental import pallas as pl
from jax.experimental.pallas import tpu as pltpu
from jax.sharding import PartitionSpec as P

MESH = pl.DeviceIdType.MESH
POCKETS = 16
BF = jnp.bfloat16
F32 = jnp.float32
MIB = 1 << 20
CHUNKS = 4
UNITS = 224
SLICE = 896
PIECE = 128
GATE, UP, BACK = 0, 1, 2
LEVELS = 32767.0
TINY = 1e-30


def mod4(v):
    return lax.rem(v + 4, 4)


class Sems:
    def __init__(self, ref):
        self.ref, self.used = ref, 0

    def take(self, count=1):
        base = self.used
        self.used += count
        return base


def kernel(
    tok, grd, gate_h, up_h, down_h, ids_ref,
    act_o, grad_o, hid_o, gg_o, ug_o,
    xt, wg, wu, wd, pbuf, rbuf, xsend, xrecv, tsend, trecv, vw, sb, cols, stage, res, wrow, wcol,
    ssem, rsem, lsem,
):
    dp = lax.axis_index("dp")
    tensor = lax.axis_index("tensor")
    xh, y, z = dp // 16, (dp // 4) % 4, dp % 4
    xl, c = tensor // 2, tensor % 2
    e = dp % 8

    def dev(xh_, y_, z_, xl_, c_):
        return {"dp": xh_ * 16 + y_ * 4 + z_, "tensor": xl_ * 2 + c_}

    sibling = dev(xh, y, z, xl, 1 - c)
    partner = dev(xh, y, z, 1 - xl, c)
    twin = dev(1 - xh, y, z, xl, c)
    y_peer = [dev(xh, mod4(y + s), z, xl, c) for s in (1, 2, 3)]
    z_peer = [dev(xh, y, mod4(z + s), xl, c) for s in (1, 2, 3)]
    around = [{"dp": lax.rem(dp + s, 32), "tensor": t} for s in (1, 31) for t in range(4)]
    above, below = ({"dp": lax.rem(dp + s, 32), "tensor": tensor} for s in (1, 31))
    across = [dev(1 - xh, y, z, 1 - xl, k) for k in (0, 1)]

    send, recv, here = Sems(ssem), Sems(rsem), Sems(lsem)
    groups = {}

    def push(src, dst, to, r, group):
        s = groups.setdefault(group, None)
        if s is None:
            s = groups[group] = send.take()
        copy = pltpu.make_async_remote_copy(
            src_ref=src, dst_ref=dst, send_sem=ssem.at[s], recv_sem=rsem.at[r],
            device_id=to, device_id_type=MESH,
        )
        copy.start()
        return copy

    def group_sent(group, ref):
        pltpu.make_async_copy(ref, ref, ssem.at[groups.pop(group)]).wait()

    def arrived(ref, r):
        pltpu.make_async_copy(ref, ref, rsem.at[r]).wait()

    def stay(src, dst):
        copy = pltpu.make_async_copy(src, dst, lsem.at[here.take()])
        copy.start()
        return copy

    shard = (tok, grd)
    pkg_of = (y, 4 + z)
    inner = (xh * 64 + z * 16, xh * 64 + y * 16)
    twin_inner = ((1 - xh) * 64 + z * 16, (1 - xh) * 64 + y * 16)

    def rows16(ref, a, half, start):
        return ref.at[a, pkg_of[half], pl.ds(pl.multiple_of(start, 16), 16)]

    own_copies = [
        [stay(shard[a].at[pl.ds(16 * h, 16)], rows16(xt, a, h, inner[h])) for h in (0, 1)]
        for a in (0, 1)
    ]
    weight_copies = [stay(gate_h, wg), stay(up_h, wu), stay(down_h, wd)]

    def pocket_weights():
        ids = ids_ref[...]
        weights = jnp.zeros((8, 128), F32)
        for k in range(POCKETS):
            member = (ids == k).astype(F32)
            count = jnp.sum(jnp.sum(member, axis=1, keepdims=True), axis=0, keepdims=True)
            weights = weights + member * (1.0 / (POCKETS * count))
        for p in range(8):
            wrow[p] = weights[p : p + 1]
        wcol[...] = weights.T

    pocket_weights()

    barrier = pltpu.get_barrier_semaphore()
    greeted = [sibling, partner, twin, *y_peer, *z_peer, *across, *around]
    for peer in greeted:
        pl.semaphore_signal(barrier, inc=1, device_id=peer, device_id_type=MESH)
    pl.semaphore_wait(barrier, len(greeted))

    twin_sem = [[recv.take() for _ in (0, 1)] for _ in (0, 1)]
    ring_sem = [[recv.take() for _ in (0, 1)] for _ in (0, 1)]
    ring_peer = (z_peer, y_peer)
    def start_twin(a):
        for h in (0, 1):
            push(shard[a].at[pl.ds(16 * h, 16)], rows16(xt, a, h, inner[h]), twin, twin_sem[a][h], "twin")

    def start_ring(a):
        for h in (0, 1):
            for peer in ring_peer[h]:
                push(shard[a].at[pl.ds(16 * h, 16)], rows16(xt, a, h, inner[h]), peer, ring_sem[a][h], "ring")

    def forward_twin(a):
        for h in (0, 1):
            piece = rows16(xt, a, h, twin_inner[h])
            arrived(piece, twin_sem[a][h])
            for peer in ring_peer[h]:
                push(piece, piece, peer, ring_sem[a][h], "ring")

    side_peer = ((y_peer[2], y_peer[0]), (z_peer[2], z_peer[0]))
    side_sem = [[[recv.take() for _ in (0, 1)] for _ in (0, 1)] for _ in (0, 1)]
    far_sem = [[[recv.take() for _ in (0, 1)] for _ in (0, 1)] for _ in (0, 1)]
    coord = (y, z)

    def package(h, step):
        return 4 * h + mod4(coord[h] + step)

    def send_packages(a):
        for h in (0, 1):
            own_copies[a][h].wait()
            arrived(xt.at[a, pkg_of[h], pl.ds(0, 96)], ring_sem[a][h])
            whole = xt.at[a, pkg_of[h]]
            for s in (0, 1):
                push(whole, whole, side_peer[h][s], side_sem[a][h][1 - s], "side")

    def forward_packages(a):
        for h in (0, 1):
            for s in (0, 1):
                whole = xt.at[a, package(h, (-1, 1)[s])]
                arrived(whole, side_sem[a][h][s])
                part = xt.at[a, package(h, (-1, 1)[s]), pl.ds(64 * s, 64)]
                push(part, part, side_peer[h][1 - s], far_sem[a][h][s], "far")

    def far_packages(a):
        for h in (0, 1):
            for s in (0, 1):
                arrived(xt.at[a, package(h, 2), pl.ds(64 * s, 64)], far_sem[a][h][s])

    chunk_pkgs = [
        (package(0, 0), package(1, 0)),
        (package(0, -1), package(0, 1)),
        (package(1, -1), package(1, 1)),
        (package(0, 2), package(1, 2)),
    ]

    def pkgs_of(k, y_, z_):
        return [
            (y_, 4 + z_),
            (mod4(y_ - 1), mod4(y_ + 1)),
            (4 + mod4(z_ - 1), 4 + mod4(z_ + 1)),
            (mod4(y_ + 2), 4 + mod4(z_ + 2)),
        ][k]

    core_sem = [[recv.take() for _ in range(3)] for _ in range(CHUNKS)]
    line_sem = [[recv.take() for _ in range(3)] for _ in range(CHUNKS)]
    top_sem = [[recv.take() for _ in range(3)] for _ in range(CHUNKS)]
    slot_of = {}
    slot_sent = [None] * 3
    weights_in = [False] * 3

    def project(k, m):
        if not weights_in[m]:
            weight_copies[m].wait()
            weights_in[m] = True
        slot = len(slot_of) % 3
        assert slot not in busy.values()
        a = 1 if m == BACK else 0
        x = jnp.concatenate([xt[a, chunk_pkgs[k][0]], xt[a, chunk_pkgs[k][1]]], axis=0)
        if m == BACK:
            part = lax.dot_general(wd[...], x, (((1,), (1,)), ((), ())), preferred_element_type=F32)
        else:
            w = (wg, wu)[m]
            part = lax.dot_general(w[...], x, (((0,), (1,)), ((), ())), preferred_element_type=F32)
        if slot_sent[slot] is not None:
            slot_sent[slot].wait_send()
        for i in range(4):
            pbuf[slot, i // 2, i % 2] = part[UNITS * i : UNITS * (i + 1)]
        slot_sent[slot] = push(pbuf.at[slot, :, 1 - c], rbuf.at[k, m], sibling, core_sem[k][m], slot)
        slot_of[k, m] = slot
        busy[k, m] = slot

    busy = {}

    def combine(k, m):
        slot = busy.pop((k, m))
        arrived(rbuf.at[k, m], core_sem[k][m])

        def add(i, top):
            r = pl.ds(pl.multiple_of(i * 32, 32), 32)
            value = rbuf[k, m, 1 - xl, r] + pbuf[slot, 1 - xl, c, r]
            rbuf[k, m, 1 - xl, r] = value
            rbuf[k, m, xl, r] = rbuf[k, m, xl, r] + pbuf[slot, xl, c, r]
            return jnp.maximum(top, jnp.abs(value))

        top = lax.fori_loop(0, UNITS // 32, add, jnp.zeros((32, 256), F32))
        top = jnp.max(top, axis=0, keepdims=True)
        tsend[k, m] = top
        scale = jnp.where(top > TINY, 1.0 / jnp.maximum(top, TINY), 0.0)

        def code(i, _):
            r = pl.ds(pl.multiple_of(i * 32, 32), 32)
            value = rbuf[k, m, 1 - xl, r]
            share = jnp.abs(value) * scale
            root = share * lax.rsqrt(jnp.maximum(share, TINY))
            level = (root * LEVELS + 0.5).astype(jnp.int32)
            xsend[k, m, r] = jnp.where(value < 0, -level, level).astype(jnp.int16)
            return 0

        lax.fori_loop(0, UNITS // 32, code, 0)
        push(tsend.at[k, m], trecv.at[k, m], partner, top_sem[k][m], "top")
        push(xsend.at[k, m], xrecv.at[k, m], partner, line_sem[k][m], "line")

    base = 1024 - PIECE * e

    def rows_of(t):
        return pl.ds(pl.multiple_of(base + UNITS * t, 32), UNITS)

    part_of = (pl.ds(0, 1), pl.ds(1, 2))
    arrays_of = ((0,), (1, 2))
    own_sem, cross_sem, relay_sem = (
        [[recv.take(2) for _ in (0, 1)] for _ in range(CHUNKS)] for _ in range(3)
    )

    def units(part, k, q, t):
        return vw.at[part_of[part], chunk_pkgs[k][q], rows_of(t)]

    def finish(k, part):
        for m in (GATE, UP) if part == 0 else (BACK,):
            arrived(trecv.at[k, m], top_sem[k][m])
            arrived(xrecv.at[k, m], line_sem[k][m])

        def total(m, r):
            root = xrecv[k, m, r].astype(F32) * (1.0 / LEVELS)
            return rbuf[k, m, xl, r] + root * jnp.abs(root) * trecv[k, m]

        def body(i, _):
            r = pl.ds(pl.multiple_of(i * 32, 32), 32)
            gate, up = total(GATE, r), total(UP, r)
            sig = 1.0 / (1.0 + jnp.exp(-gate))
            activated = gate * sig
            if part == 0:
                values = ((0, activated * up),)
            else:
                back = total(BACK, r)
                values = ((1, back * up * sig * (1.0 + gate * (1.0 - sig))), (2, back * activated))
            wr = pl.ds(pl.multiple_of(base + UNITS * tensor + i * 32, 32), 32)
            for j, value in values:
                value = value.astype(BF)
                for q in (0, 1):
                    p = chunk_pkgs[k][q]
                    v = value[:, 128 * q : 128 * (q + 1)]
                    vw[j, p, wr] = v
                    sb[j, p, r] = (v.astype(F32) * wrow[p]).astype(BF)
            return 0

        lax.fori_loop(0, UNITS // 32, body, 0)
        for q in (0, 1):
            mine = units(part, k, q, tensor)
            push(mine, mine, partner, cross_sem[k][part] + q, "cross")
        for q in (0, 1):
            mine = units(part, k, q, tensor)
            push(mine, mine, sibling, own_sem[k][part] + q, "own")

    def relay(k, part, q):
        theirs = units(part, k, q, (1 - xl) * 2 + c)
        arrived(theirs, cross_sem[k][part] + q)
        push(theirs, theirs, sibling, relay_sem[k][part] + q, "relay")

    def package_ready(k, part, q):
        p = jnp.where(q == 0, *chunk_pkgs[k])
        for t, sem in ((xl * 2 + 1 - c, own_sem), ((1 - xl) * 2 + 1 - c, relay_sem)):
            arrived(vw.at[part_of[part], p, rows_of(t)], sem[k][part] + q)

    low = e <= 3
    n_down = jnp.where(e <= 4, e, 0)
    n_up = jnp.where(jnp.logical_and(e >= 3, e <= 6), 7 - e, 0)
    n_near = jnp.where(low, e + 1, 8 - e)
    near_row = jnp.where(low, base + SLICE, 0)
    near_dp = jnp.where(low, dp + 1, dp + 31)
    near_y, near_z = (near_dp // 4) % 4, near_dp % 4
    my_pkg = [jnp.where(c == 0, *chunk_pkgs[k]) for k in range(CHUNKS)]
    near_pkg = [jnp.where(c == 0, *pkgs_of(k, near_y, near_z)) for k in range(CHUNKS)]
    near_sem, near_relay = ([recv.take(2) for _ in range(CHUNKS)] for _ in range(2))
    down_send, up_send, near_send = ([send.take(2) for _ in range(CHUNKS)] for _ in range(3))

    def sized(count, most, f):
        for n in range(1, most + 1):
            pl.when(count == n)(functools.partial(f, n))

    def win(part, p, row, n):
        return vw.at[part_of[part], p, pl.ds(pl.multiple_of(row, PIECE), n * PIECE)]

    def down_copy(k, part, n):
        return pltpu.make_async_remote_copy(
            src_ref=win(part, my_pkg[k], base, n), dst_ref=win(part, my_pkg[k], base + 1024, n),
            send_sem=ssem.at[down_send[k] + part], recv_sem=rsem.at[near_sem[k] + part],
            device_id=below, device_id_type=MESH,
        )

    def up_copy(k, part, n):
        return pltpu.make_async_remote_copy(
            src_ref=win(part, my_pkg[k], base + PIECE * e, n), dst_ref=win(part, my_pkg[k], 0, n),
            send_sem=ssem.at[up_send[k] + part], recv_sem=rsem.at[near_sem[k] + part],
            device_id=above, device_id_type=MESH,
        )

    def near_copy(k, part, n):
        ref = win(part, near_pkg[k], near_row, n)
        return pltpu.make_async_remote_copy(
            src_ref=ref, dst_ref=ref, send_sem=ssem.at[near_send[k] + part], recv_sem=rsem.at[near_relay[k] + part],
            device_id=sibling, device_id_type=MESH,
        )

    def pass_on(k, part):
        for q in (0, 1):
            relay(k, part, q)

            @pl.when(c == q)
            def _():
                package_ready(k, part, q)
                sized(n_down, 4, lambda n: down_copy(k, part, n).start())
                sized(n_up, 4, lambda n: up_copy(k, part, n).start())

    def relay_neighbours(k, part):
        def go(n):
            arrived(win(part, near_pkg[k], near_row, n), near_sem[k] + part)
            near_copy(k, part, n).start()

        sized(n_near, 4, go)

    def units_complete(k, part):
        package_ready(k, part, 1 - c)
        sized(n_near, 4, lambda n: arrived(win(part, near_pkg[k], near_row, n), near_relay[k] + part))

    def neighbours_sent(k, part):
        sized(n_down, 4, lambda n: down_copy(k, part, n).wait_send())
        sized(n_up, 4, lambda n: up_copy(k, part, n).wait_send())
        sized(n_near, 4, lambda n: near_copy(k, part, n).wait_send())

    major = jnp.logical_or(e <= 2, e >= 5)
    n_cols = jnp.where(low, 7 - e, e)
    first_col = jnp.where(low, e, 0)
    res_sem = recv.take(16)
    res_send = send.take(48)
    pair = (tensor, tensor + 4)

    def result_copy(part, i, r, h):
        row = jnp.where(low, 0, PIECE * (e - 1)) + PIECE * i + 32 * r
        owner = row // UNITS
        col = jnp.where(low, 0, 8 - e) + pair[h]
        return pltpu.make_async_remote_copy(
            src_ref=stage.at[part_of[part], i, pl.ds(32 * r, 32), pl.ds(128 * h, 128)],
            dst_ref=res.at[
                part_of[part],
                pl.ds(pl.multiple_of(row - UNITS * owner, 32), 32),
                pl.ds(pl.multiple_of(128 * col, 128), 128),
            ],
            send_sem=ssem.at[res_send + 24 * part + 8 * i + 2 * r + h], recv_sem=rsem.at[res_sem + 8 * part + col],
            device_id={"dp": near_dp % 32, "tensor": owner}, device_id_type=MESH,
        )

    def each_result(part, i, f):
        for h in (0, 1):
            @pl.when(pair[h] < n_cols)
            def _():
                for r in range(4):
                    f(result_copy(part, i, r, h))

    def products_for_neighbour(part):
        def body(i, _):
            rows = pl.ds(pl.multiple_of(near_row + PIECE * i, PIECE), PIECE)
            cols_at = [
                pl.ds(pl.multiple_of(base + PIECE * (first_col + jnp.minimum(piece, n_cols - 1)), PIECE), PIECE)
                for piece in pair
            ]
            for j in arrays_of[part]:
                lhs = jnp.concatenate(
                    [(vw[j, p, rows].astype(F32) * wrow[p]).astype(BF) for p in range(8)], axis=1
                )
                rhs = jnp.concatenate(
                    [jnp.concatenate([vw[j, p, at] for at in cols_at], axis=0) for p in range(8)], axis=1
                )
                stage[j, i] = lax.dot_general(
                    lhs, rhs, (((1,), (1,)), ((), ())), preferred_element_type=F32
                ).astype(BF)
            each_result(part, i, lambda copy: copy.start())
            return 0

        @pl.when(major)
        def _():
            lax.fori_loop(0, n_near, body, 0)

    def products_sent():
        def body(i, _):
            for part in (0, 1):
                each_result(part, i, lambda copy: copy.wait_send())
            return 0

        @pl.when(major)
        def _():
            lax.fori_loop(0, n_near, body, 0)

    col_sem = [recv.take() for _ in (0, 1)]
    col_send = [send.take(2) for _ in (0, 1)]
    col_here = [here.take() for _ in (0, 1)]
    holder = c == y // 2
    at_home = xl == xh
    col_start = pl.multiple_of(e * 256, 256)

    def col_copies(a):
        src = xt.at[a, :, :, pl.ds(col_start, 256)]
        make = lambda to, i: pltpu.make_async_remote_copy(
            src_ref=src, dst_ref=cols.at[a], send_sem=ssem.at[col_send[a] + i], recv_sem=rsem.at[col_sem[a]],
            device_id=to, device_id_type=MESH,
        )
        return make(sibling, 0), make(across[0], 0), make(across[1], 1), pltpu.make_async_copy(
            src, cols.at[a], lsem.at[col_here[a]]
        )

    home_holder = jnp.logical_and(holder, at_home)
    far_holder = jnp.logical_and(holder, jnp.logical_not(at_home))

    def send_cols(a):
        home, far0, far1, local = col_copies(a)

        @pl.when(home_holder)
        def _():
            home.start()
            local.start()

        @pl.when(far_holder)
        def _():
            far0.start()
            far1.start()

    def cols_complete(a):
        _, _, _, local = col_copies(a)

        @pl.when(home_holder)
        def _():
            local.wait()

        @pl.when(jnp.logical_not(home_holder))
        def _():
            arrived(cols.at[a], col_sem[a])

    def cols_sent(a):
        home, far0, far1, _ = col_copies(a)

        @pl.when(home_holder)
        def _():
            home.wait_send()

        @pl.when(far_holder)
        def _():
            far0.wait_send()
            far1.wait_send()

    cov_out = (act_o, grad_o)

    def full_cov(a):
        rhs = cols[a].reshape(1024, 256)

        def body(i, _):
            k = pl.ds(pl.multiple_of(i * 256, 256), 256)
            parts = [
                (xt[a, p, :, k].astype(F32) * wcol[:, p : p + 1]).astype(BF) for p in range(8)
            ]
            cov_out[a][k] = lax.dot_general(
                jnp.concatenate(parts, axis=0), rhs, (((0,), (0,)), ((), ())), preferred_element_type=F32
            )
            return 0

        lax.fori_loop(0, 8, body, 0)

    split_row = jnp.clip(PIECE * e - UNITS * tensor, 0, UNITS)
    has_early, has_late = split_row > 0, split_row < UNITS
    blk_out = (hid_o, gg_o, ug_o)

    def block_cov(part):
        row = lax.broadcasted_iota(jnp.int32, (UNITS, 256), 0)

        def body(g, _):
            k = pl.multiple_of(g * 256, 256)

            def product(j, start):
                lhs = jnp.concatenate([sb[j, p] for p in range(8)], axis=1)
                rhs = jnp.concatenate([vw[j, p, pl.ds(start + k, 256)] for p in range(8)], axis=1)
                return lax.dot_general(lhs, rhs, (((1,), (1,)), ((), ())), preferred_element_type=F32)

            @pl.when(jnp.logical_and(has_late, jnp.logical_or(low, 2 * g <= 6 - e)))
            def _():
                for j in arrays_of[part]:
                    blk_out[j][:, pl.ds(k, 256)] = product(j, 1024)

            @pl.when(jnp.logical_and(has_early, jnp.logical_or(jnp.logical_not(low), 2 * g + 1 >= 8 - e)))
            def _():
                for j in arrays_of[part]:
                    blk_out[j][:, pl.ds(k, 256)] = jnp.where(
                        row < split_row, product(j, 0), blk_out[j][:, pl.ds(k, 256)]
                    )

            return 0

        lax.fori_loop(0, 4, body, 0)

    def products_from_neighbour(part):
        row = lax.broadcasted_iota(jnp.int32, (UNITS, 128), 0)
        minor_early = jnp.logical_and(jnp.logical_and(low, e >= 1), has_early)
        minor_late = jnp.logical_and(jnp.logical_and(jnp.logical_not(low), e <= 6), has_late)
        bands = jnp.where(low, split_row, UNITS - split_row) // 32
        start = jnp.where(low, 0, 7 - e)
        stop = jnp.where(low, 8 - e, 8)
        from_row = jnp.where(low, 0, split_row)
        to_row = jnp.where(low, split_row, UNITS)

        def body(col, _):
            sized(bands, 7, lambda n: arrived(res.at[part_of[part], pl.ds(0, 32 * n), pl.ds(0, 128)], res_sem + 8 * part + col))
            at = pl.ds(pl.multiple_of(col * 128, 128), 128)
            here_too = jnp.logical_and(row >= from_row, row < to_row)
            for j in arrays_of[part]:
                blk_out[j][:, at] = jnp.where(here_too, res[j, :, at].astype(F32), blk_out[j][:, at])
            return 0

        @pl.when(jnp.logical_or(minor_early, minor_late))
        def _():
            lax.fori_loop(start, stop, body, 0)

    start_twin(0)
    start_ring(0)
    start_twin(1)
    forward_twin(0)
    start_ring(1)
    forward_twin(1)
    send_packages(0)
    project(0, GATE)
    project(0, UP)
    combine(0, GATE)
    send_packages(1)
    project(0, BACK)
    combine(0, UP)
    combine(0, BACK)
    finish(0, 0)
    forward_packages(0)
    project(1, GATE)
    project(1, UP)
    combine(1, GATE)
    project(2, GATE)
    combine(1, UP)
    project(2, UP)
    combine(2, GATE)
    combine(2, UP)
    finish(0, 1)
    forward_packages(1)
    project(1, BACK)
    project(2, BACK)
    combine(1, BACK)
    combine(2, BACK)
    finish(1, 0)
    finish(2, 0)
    pass_on(0, 0)
    far_packages(0)
    send_cols(0)
    project(3, GATE)
    project(3, UP)
    combine(3, GATE)
    combine(3, UP)
    pass_on(0, 1)
    finish(1, 1)
    finish(2, 1)
    far_packages(1)
    send_cols(1)
    project(3, BACK)
    combine(3, BACK)
    finish(3, 0)
    pass_on(1, 0)
    pass_on(2, 0)
    pass_on(1, 1)
    pass_on(2, 1)
    relay_neighbours(0, 0)
    relay_neighbours(0, 1)
    finish(3, 1)
    cols_complete(0)
    full_cov(0)
    pass_on(3, 0)
    relay_neighbours(1, 0)
    relay_neighbours(2, 0)
    pass_on(3, 1)
    relay_neighbours(3, 0)
    relay_neighbours(1, 1)
    relay_neighbours(2, 1)
    for k in range(CHUNKS):
        units_complete(k, 0)
    products_for_neighbour(0)
    block_cov(0)
    relay_neighbours(3, 1)
    for k in range(CHUNKS):
        units_complete(k, 1)
    products_for_neighbour(1)
    cols_complete(1)
    full_cov(1)
    block_cov(1)
    products_from_neighbour(0)
    products_from_neighbour(1)
    for copy in slot_sent:
        copy.wait_send()
    group_sent("twin", xt.at[0, 0, pl.ds(0, 64)])
    group_sent("ring", xt.at[0, pl.ds(0, 3)])
    group_sent("side", xt.at[0])
    group_sent("far", xt.at[0, pl.ds(0, 4)])
    group_sent("top", tsend)
    group_sent("line", xsend)
    group_sent("cross", sb)
    group_sent("own", sb)
    group_sent("relay", sb)
    for k in range(CHUNKS):
        for part in (0, 1):
            neighbours_sent(k, part)
    for a in (0, 1):
        cols_sent(a)
    products_sent()
    assert (send.used, recv.used, here.used) == (N_SEND, N_RECV, N_LOCAL)


N_SEND, N_RECV, N_LOCAL = 88, 142, 9


def write_out(*refs):
    sources, targets, sems = refs[:5], refs[5:10], refs[10]
    copies = [pltpu.make_async_copy(a, b, sems.at[i]) for i, (a, b) in enumerate(zip(sources, targets))]
    for copy in copies:
        copy.start()
    for copy in copies:
        copy.wait()


def local(tokens, out_grad, gate_weight, up_weight, down_weight, pocket_ids):
    ids = pocket_ids.reshape(2, 4, 4, 2, 16)
    ids = jnp.concatenate(
        [
            ids[:, :, :, 0].transpose(1, 0, 2, 3).reshape(4, 128),
            ids[:, :, :, 1].transpose(2, 0, 1, 3).reshape(4, 128),
        ]
    )
    any_spec = pl.BlockSpec(memory_space=pl.ANY)
    vmem = pl.BlockSpec(memory_space=pltpu.VMEM)
    factors = pl.pallas_call(
        kernel,
        out_shape=[
            pltpu.VMEM((2048, 256), F32),
            pltpu.VMEM((2048, 256), F32),
            pltpu.VMEM((UNITS, 1024), F32),
            pltpu.VMEM((UNITS, 1024), F32),
            pltpu.VMEM((UNITS, 1024), F32),
        ],
        in_specs=[any_spec] * 5 + [vmem],
        out_specs=[vmem] * 5,
        scratch_shapes=[
            pltpu.VMEM((2, 8, 128, 2048), BF),
            pltpu.VMEM((2048, SLICE), BF),
            pltpu.VMEM((2048, SLICE), BF),
            pltpu.VMEM((SLICE, 2048), BF),
            pltpu.VMEM((3, 2, 2, UNITS, 256), F32),
            pltpu.VMEM((CHUNKS, 3, 2, UNITS, 256), F32),
            pltpu.VMEM((CHUNKS, 3, UNITS, 256), jnp.int16),
            pltpu.VMEM((CHUNKS, 3, UNITS, 256), jnp.int16),
            pltpu.VMEM((CHUNKS, 3, 1, 256), F32),
            pltpu.VMEM((CHUNKS, 3, 1, 256), F32),
            pltpu.VMEM((3, 8, 2048, 128), BF),
            pltpu.VMEM((3, 8, UNITS, 128), BF),
            pltpu.VMEM((2, 8, 128, 256), BF),
            pltpu.VMEM((3, 3, 128, 256), BF),
            pltpu.VMEM((3, UNITS, 1024), BF),
            pltpu.VMEM((8, 1, 128), F32),
            pltpu.VMEM((128, 8), F32),
            pltpu.SemaphoreType.DMA((N_SEND,)),
            pltpu.SemaphoreType.DMA((N_RECV,)),
            pltpu.SemaphoreType.DMA((N_LOCAL,)),
        ],
        compiler_params=pltpu.CompilerParams(
            collective_id=0, has_side_effects=True, vmem_limit_bytes=52 * MIB
        ),
        name="ekfac_factors",
    )(tokens, out_grad, gate_weight, up_weight, down_weight, ids)
    return pl.pallas_call(
        write_out,
        out_shape=[jax.ShapeDtypeStruct(factor.shape, F32) for factor in factors],
        in_specs=[vmem] * 5,
        out_specs=[any_spec] * 5,
        scratch_shapes=[pltpu.SemaphoreType.DMA((5,))],
        compiler_params=pltpu.CompilerParams(vmem_limit_bytes=4 * MIB),
        name="write_factors",
    )(*(pltpu.with_memory_space_constraint(factor, pltpu.VMEM) for factor in factors))


def solution(mesh):
    return jax.shard_map(
        local,
        mesh=mesh,
        in_specs=(
            P("dp", "tensor"),
            P("dp", "tensor"),
            P("tensor", "dp"),
            P("tensor", "dp"),
            P("dp", "tensor"),
            P(),
        ),
        out_specs=(
            P("tensor", "dp"),
            P("tensor", "dp"),
            P(("dp", "tensor"), None),
            P(("dp", "tensor"), None),
            P(("dp", "tensor"), None),
        ),
        check_vma=False,
    )
```

```python
import functools

import jax
import jax.numpy as jnp
from jax import lax
from jax.experimental import pallas as pl
from jax.experimental.pallas import tpu as pltpu
from jax.sharding import PartitionSpec as P

MESH = pl.DeviceIdType.MESH
POCKETS = 16
BF = jnp.bfloat16
F32 = jnp.float32
MIB = 1 << 20
CHUNKS = 4
UNITS = 224
SLICE = 896
PIECE = 128
GATE, UP, BACK = 0, 1, 2
LEVELS = 32767.0
TINY = 1e-30


def mod4(v):
    return lax.rem(v + 4, 4)


class Sems:
    def __init__(self, ref):
        self.ref, self.used = ref, 0

    def take(self, count=1):
        base = self.used
        self.used += count
        return base


def kernel(
    tok, grd, gate_h, up_h, down_h, ids_ref,
    act_o, grad_o, hid_o, gg_o, ug_o,
    xt, wg, wu, wd, pbuf, rbuf, xsend, xrecv, tsend, trecv, vw, sb, cols, stage, res, wrow, wcol,
    ssem, rsem, lsem,
):
    dp = lax.axis_index("dp")
    tensor = lax.axis_index("tensor")
    xh, y, z = dp // 16, (dp // 4) % 4, dp % 4
    xl, c = tensor // 2, tensor % 2
    e = dp % 8

    def dev(xh_, y_, z_, xl_, c_):
        return {"dp": xh_ * 16 + y_ * 4 + z_, "tensor": xl_ * 2 + c_}

    sibling = dev(xh, y, z, xl, 1 - c)
    partner = dev(xh, y, z, 1 - xl, c)
    twin = dev(1 - xh, y, z, xl, c)
    y_peer = [dev(xh, mod4(y + s), z, xl, c) for s in (1, 2, 3)]
    z_peer = [dev(xh, y, mod4(z + s), xl, c) for s in (1, 2, 3)]
    around = [{"dp": lax.rem(dp + s, 32), "tensor": t} for s in (1, 31) for t in range(4)]
    above, below = ({"dp": lax.rem(dp + s, 32), "tensor": tensor} for s in (1, 31))
    across = [dev(1 - xh, y, z, 1 - xl, k) for k in (0, 1)]

    send, recv, here = Sems(ssem), Sems(rsem), Sems(lsem)
    groups = {}

    def push(src, dst, to, r, group):
        s = groups.setdefault(group, None)
        if s is None:
            s = groups[group] = send.take()
        copy = pltpu.make_async_remote_copy(
            src_ref=src, dst_ref=dst, send_sem=ssem.at[s], recv_sem=rsem.at[r],
            device_id=to, device_id_type=MESH,
        )
        copy.start()
        return copy

    def group_sent(group, ref):
        pltpu.make_async_copy(ref, ref, ssem.at[groups.pop(group)]).wait()

    def arrived(ref, r):
        pltpu.make_async_copy(ref, ref, rsem.at[r]).wait()

    def stay(src, dst):
        copy = pltpu.make_async_copy(src, dst, lsem.at[here.take()])
        copy.start()
        return copy

    shard = (tok, grd)
    pkg_of = (y, 4 + z)
    inner = (xh * 64 + z * 16, xh * 64 + y * 16)
    twin_inner = ((1 - xh) * 64 + z * 16, (1 - xh) * 64 + y * 16)

    def rows16(ref, a, half, start):
        return ref.at[a, pkg_of[half], pl.ds(pl.multiple_of(start, 16), 16)]

    own_copies = [
        [stay(shard[a].at[pl.ds(16 * h, 16)], rows16(xt, a, h, inner[h])) for h in (0, 1)]
        for a in (0, 1)
    ]
    weight_copies = [stay(gate_h, wg), stay(up_h, wu), stay(down_h, wd)]

    def pocket_weights():
        ids = ids_ref[...]
        weights = jnp.zeros((8, 128), F32)
        for k in range(POCKETS):
            member = (ids == k).astype(F32)
            count = jnp.sum(jnp.sum(member, axis=1, keepdims=True), axis=0, keepdims=True)
            weights = weights + member * (1.0 / (POCKETS * count))
        band = lax.broadcasted_iota(jnp.int32, (8, 128), 1) // 16

        def picked(start, at):
            return jnp.where(band == at, pltpu.roll(weights, (16 * (at - start)) % 128, 1), 0.0)

        halves = jnp.zeros((4, 128), F32)
        for at in range(8):
            h = at // 4
            halves = halves + picked(2 * (at % 4), at)[4 * h : 4 * h + 4]
        packages = [halves]
        for k in range(4):
            packages.append(sum(picked(2 * k + 1, at)[at : at + 1] for at in range(8)))
        ordered = jnp.concatenate(packages, axis=0)
        for p in range(8):
            wrow[p] = ordered[p : p + 1]
        wcol[...] = ordered.T

    pocket_weights()

    barrier = pltpu.get_barrier_semaphore()
    greeted = [sibling, partner, twin, *y_peer, *z_peer, *across, *around]
    for peer in greeted:
        pl.semaphore_signal(barrier, inc=1, device_id=peer, device_id_type=MESH)
    pl.semaphore_wait(barrier, len(greeted))

    twin_sem = [[recv.take() for _ in (0, 1)] for _ in (0, 1)]
    ring_sem = [[recv.take() for _ in (0, 1)] for _ in (0, 1)]
    ring_peer = (z_peer, y_peer)
    def start_twin(a):
        for h in (0, 1):
            push(shard[a].at[pl.ds(16 * h, 16)], rows16(xt, a, h, inner[h]), twin, twin_sem[a][h], "twin")

    def start_ring(a):
        for h in (0, 1):
            for peer in ring_peer[h]:
                push(shard[a].at[pl.ds(16 * h, 16)], rows16(xt, a, h, inner[h]), peer, ring_sem[a][h], "ring")

    def forward_twin(a):
        for h in (0, 1):
            piece = rows16(xt, a, h, twin_inner[h])
            arrived(piece, twin_sem[a][h])
            for peer in ring_peer[h]:
                push(piece, piece, peer, ring_sem[a][h], "ring")

    side_peer = ((y_peer[2], y_peer[0]), (z_peer[2], z_peer[0]))
    side_sem = [[[recv.take() for _ in (0, 1)] for _ in (0, 1)] for _ in (0, 1)]
    far_sem = [[[recv.take() for _ in (0, 1)] for _ in (0, 1)] for _ in (0, 1)]
    coord = (y, z)

    def package(h, step):
        return 4 * h + mod4(coord[h] + step)

    def send_packages(a):
        for h in (0, 1):
            own_copies[a][h].wait()
            arrived(xt.at[a, pkg_of[h], pl.ds(0, 96)], ring_sem[a][h])
            whole = xt.at[a, pkg_of[h]]
            for s in (0, 1):
                push(whole, whole, side_peer[h][s], side_sem[a][h][1 - s], "side")

    def forward_packages(a):
        for h in (0, 1):
            for s in (0, 1):
                whole = xt.at[a, package(h, (-1, 1)[s])]
                arrived(whole, side_sem[a][h][s])
                part = xt.at[a, package(h, (-1, 1)[s]), pl.ds(64 * s, 64)]
                push(part, part, side_peer[h][1 - s], far_sem[a][h][s], "far")

    def far_packages(a):
        for h in (0, 1):
            for s in (0, 1):
                arrived(xt.at[a, package(h, 2), pl.ds(64 * s, 64)], far_sem[a][h][s])

    chunk_pkgs = [
        (package(0, 0), package(1, 0)),
        (package(0, -1), package(0, 1)),
        (package(1, -1), package(1, 1)),
        (package(0, 2), package(1, 2)),
    ]

    def pkgs_of(k, y_, z_):
        return [
            (y_, 4 + z_),
            (mod4(y_ - 1), mod4(y_ + 1)),
            (4 + mod4(z_ - 1), 4 + mod4(z_ + 1)),
            (mod4(y_ + 2), 4 + mod4(z_ + 2)),
        ][k]

    core_sem = [[recv.take() for _ in range(3)] for _ in range(CHUNKS)]
    line_sem = [[recv.take() for _ in range(3)] for _ in range(CHUNKS)]
    top_sem = [[recv.take() for _ in range(3)] for _ in range(CHUNKS)]
    slot_of = {}
    slot_sent = [None] * 3
    weights_in = [False] * 3

    def project(k, m):
        if not weights_in[m]:
            weight_copies[m].wait()
            weights_in[m] = True
        slot = len(slot_of) % 3
        assert slot not in busy.values()
        a = 1 if m == BACK else 0
        x = jnp.concatenate([xt[a, chunk_pkgs[k][0]], xt[a, chunk_pkgs[k][1]]], axis=0)
        if m == BACK:
            part = lax.dot_general(wd[...], x, (((1,), (1,)), ((), ())), preferred_element_type=F32)
        else:
            w = (wg, wu)[m]
            part = lax.dot_general(w[...], x, (((0,), (1,)), ((), ())), preferred_element_type=F32)
        if slot_sent[slot] is not None:
            slot_sent[slot].wait_send()
        for i in range(4):
            pbuf[slot, i // 2, i % 2] = part[UNITS * i : UNITS * (i + 1)]
        slot_sent[slot] = push(pbuf.at[slot, :, 1 - c], rbuf.at[k, m], sibling, core_sem[k][m], slot)
        slot_of[k, m] = slot
        busy[k, m] = slot

    busy = {}

    def combine(k, m):
        slot = busy.pop((k, m))
        arrived(rbuf.at[k, m], core_sem[k][m])

        def add(i, top):
            r = pl.ds(pl.multiple_of(i * 32, 32), 32)
            value = rbuf[k, m, 1 - xl, r] + pbuf[slot, 1 - xl, c, r]
            rbuf[k, m, 1 - xl, r] = value
            rbuf[k, m, xl, r] = rbuf[k, m, xl, r] + pbuf[slot, xl, c, r]
            return jnp.maximum(top, jnp.abs(value))

        top = lax.fori_loop(0, UNITS // 32, add, jnp.zeros((32, 256), F32))
        top = jnp.max(top, axis=0, keepdims=True)
        tsend[k, m] = top
        scale = jnp.where(top > TINY, 1.0 / jnp.maximum(top, TINY), 0.0)

        def code(i, _):
            r = pl.ds(pl.multiple_of(i * 32, 32), 32)
            value = rbuf[k, m, 1 - xl, r]
            share = jnp.abs(value) * scale
            root = share * lax.rsqrt(jnp.maximum(share, TINY))
            level = (root * LEVELS + 0.5).astype(jnp.int32)
            xsend[k, m, r] = jnp.where(value < 0, -level, level).astype(jnp.int16)
            return 0

        lax.fori_loop(0, UNITS // 32, code, 0)
        push(tsend.at[k, m], trecv.at[k, m], partner, top_sem[k][m], "top")
        push(xsend.at[k, m], xrecv.at[k, m], partner, line_sem[k][m], "line")

    base = 1024 - PIECE * e

    def rows_of(t):
        return pl.ds(pl.multiple_of(base + UNITS * t, 32), UNITS)

    part_of = (pl.ds(0, 1), pl.ds(1, 2))
    arrays_of = ((0,), (1, 2))
    own_sem, cross_sem, relay_sem = (
        [[recv.take(2) for _ in (0, 1)] for _ in range(CHUNKS)] for _ in range(3)
    )

    def units(part, k, q, t):
        return vw.at[part_of[part], chunk_pkgs[k][q], rows_of(t)]

    def finish(k, part):
        for m in (GATE, UP) if part == 0 else (BACK,):
            arrived(trecv.at[k, m], top_sem[k][m])
            arrived(xrecv.at[k, m], line_sem[k][m])

        def total(m, r):
            root = xrecv[k, m, r].astype(F32) * (1.0 / LEVELS)
            return rbuf[k, m, xl, r] + root * jnp.abs(root) * trecv[k, m]

        def body(i, _):
            r = pl.ds(pl.multiple_of(i * 32, 32), 32)
            gate, up = total(GATE, r), total(UP, r)
            sig = 1.0 / (1.0 + jnp.exp(-gate))
            activated = gate * sig
            if part == 0:
                values = ((0, activated * up),)
            else:
                back = total(BACK, r)
                values = ((1, back * up * sig * (1.0 + gate * (1.0 - sig))), (2, back * activated))
            wr = pl.ds(pl.multiple_of(base + UNITS * tensor + i * 32, 32), 32)
            for j, value in values:
                value = value.astype(BF)
                for q in (0, 1):
                    p = chunk_pkgs[k][q]
                    v = value[:, 128 * q : 128 * (q + 1)]
                    vw[j, p, wr] = v
                    sb[j, p, r] = (v.astype(F32) * wrow[p]).astype(BF)
            return 0

        lax.fori_loop(0, UNITS // 32, body, 0)
        for q in (0, 1):
            mine = units(part, k, q, tensor)
            push(mine, mine, partner, cross_sem[k][part] + q, "cross")
        for q in (0, 1):
            mine = units(part, k, q, tensor)
            push(mine, mine, sibling, own_sem[k][part] + q, "own")

    def relay(k, part, q):
        theirs = units(part, k, q, (1 - xl) * 2 + c)
        arrived(theirs, cross_sem[k][part] + q)
        push(theirs, theirs, sibling, relay_sem[k][part] + q, "relay")

    def package_ready(k, part, q):
        p = jnp.where(q == 0, *chunk_pkgs[k])
        for t, sem in ((xl * 2 + 1 - c, own_sem), ((1 - xl) * 2 + 1 - c, relay_sem)):
            arrived(vw.at[part_of[part], p, rows_of(t)], sem[k][part] + q)

    low = e <= 3
    n_down = jnp.where(e <= 4, e, 0)
    n_up = jnp.where(jnp.logical_and(e >= 3, e <= 6), 7 - e, 0)
    n_near = jnp.where(low, e + 1, 8 - e)
    near_row = jnp.where(low, base + SLICE, 0)
    near_dp = jnp.where(low, dp + 1, dp + 31)
    near_y, near_z = (near_dp // 4) % 4, near_dp % 4
    my_pkg = [jnp.where(c == 0, *chunk_pkgs[k]) for k in range(CHUNKS)]
    near_pkg = [jnp.where(c == 0, *pkgs_of(k, near_y, near_z)) for k in range(CHUNKS)]
    near_sem, near_relay = ([recv.take(2) for _ in range(CHUNKS)] for _ in range(2))
    down_send, up_send, near_send = ([send.take(2) for _ in range(CHUNKS)] for _ in range(3))

    def sized(count, most, f):
        for n in range(1, most + 1):
            pl.when(count == n)(functools.partial(f, n))

    def win(part, p, row, n):
        return vw.at[part_of[part], p, pl.ds(pl.multiple_of(row, PIECE), n * PIECE)]

    def down_copy(k, part, n):
        return pltpu.make_async_remote_copy(
            src_ref=win(part, my_pkg[k], base, n), dst_ref=win(part, my_pkg[k], base + 1024, n),
            send_sem=ssem.at[down_send[k] + part], recv_sem=rsem.at[near_sem[k] + part],
            device_id=below, device_id_type=MESH,
        )

    def up_copy(k, part, n):
        return pltpu.make_async_remote_copy(
            src_ref=win(part, my_pkg[k], base + PIECE * e, n), dst_ref=win(part, my_pkg[k], 0, n),
            send_sem=ssem.at[up_send[k] + part], recv_sem=rsem.at[near_sem[k] + part],
            device_id=above, device_id_type=MESH,
        )

    def near_copy(k, part, n):
        ref = win(part, near_pkg[k], near_row, n)
        return pltpu.make_async_remote_copy(
            src_ref=ref, dst_ref=ref, send_sem=ssem.at[near_send[k] + part], recv_sem=rsem.at[near_relay[k] + part],
            device_id=sibling, device_id_type=MESH,
        )

    def pass_on(k, part):
        for q in (0, 1):
            relay(k, part, q)

            @pl.when(c == q)
            def _():
                package_ready(k, part, q)
                sized(n_down, 4, lambda n: down_copy(k, part, n).start())
                sized(n_up, 4, lambda n: up_copy(k, part, n).start())

    def relay_neighbours(k, part):
        def go(n):
            arrived(win(part, near_pkg[k], near_row, n), near_sem[k] + part)
            near_copy(k, part, n).start()

        sized(n_near, 4, go)

    def units_complete(k, part):
        package_ready(k, part, 1 - c)
        sized(n_near, 4, lambda n: arrived(win(part, near_pkg[k], near_row, n), near_relay[k] + part))

    def neighbours_sent(k, part):
        sized(n_down, 4, lambda n: down_copy(k, part, n).wait_send())
        sized(n_up, 4, lambda n: up_copy(k, part, n).wait_send())
        sized(n_near, 4, lambda n: near_copy(k, part, n).wait_send())

    major = jnp.logical_or(e <= 2, e >= 5)
    n_cols = jnp.where(low, 7 - e, e)
    first_col = jnp.where(low, e, 0)
    res_sem = recv.take(16)
    res_send = send.take(48)
    pair = (tensor, tensor + 4)

    def result_copy(part, i, r, h):
        row = jnp.where(low, 0, PIECE * (e - 1)) + PIECE * i + 32 * r
        owner = row // UNITS
        col = jnp.where(low, 0, 8 - e) + pair[h]
        return pltpu.make_async_remote_copy(
            src_ref=stage.at[part_of[part], i, pl.ds(32 * r, 32), pl.ds(128 * h, 128)],
            dst_ref=res.at[
                part_of[part],
                pl.ds(pl.multiple_of(row - UNITS * owner, 32), 32),
                pl.ds(pl.multiple_of(128 * col, 128), 128),
            ],
            send_sem=ssem.at[res_send + 24 * part + 8 * i + 2 * r + h], recv_sem=rsem.at[res_sem + 8 * part + col],
            device_id={"dp": near_dp % 32, "tensor": owner}, device_id_type=MESH,
        )

    def each_result(part, i, f):
        for h in (0, 1):
            @pl.when(pair[h] < n_cols)
            def _():
                for r in range(4):
                    f(result_copy(part, i, r, h))

    def products_for_neighbour(part):
        def body(i, _):
            rows = pl.ds(pl.multiple_of(near_row + PIECE * i, PIECE), PIECE)
            cols_at = [
                pl.ds(pl.multiple_of(base + PIECE * (first_col + jnp.minimum(piece, n_cols - 1)), PIECE), PIECE)
                for piece in pair
            ]
            for j in arrays_of[part]:
                lhs = jnp.concatenate(
                    [(vw[j, p, rows].astype(F32) * wrow[p]).astype(BF) for p in range(8)], axis=1
                )
                rhs = jnp.concatenate(
                    [jnp.concatenate([vw[j, p, at] for at in cols_at], axis=0) for p in range(8)], axis=1
                )
                stage[j, i] = lax.dot_general(
                    lhs, rhs, (((1,), (1,)), ((), ())), preferred_element_type=F32
                ).astype(BF)
            each_result(part, i, lambda copy: copy.start())
            return 0

        @pl.when(major)
        def _():
            lax.fori_loop(0, n_near, body, 0)

    def products_sent():
        def body(i, _):
            for part in (0, 1):
                each_result(part, i, lambda copy: copy.wait_send())
            return 0

        @pl.when(major)
        def _():
            lax.fori_loop(0, n_near, body, 0)

    col_sem = [recv.take() for _ in (0, 1)]
    col_send = [send.take(2) for _ in (0, 1)]
    col_here = [here.take() for _ in (0, 1)]
    holder = c == y // 2
    at_home = xl == xh
    col_start = pl.multiple_of(e * 256, 256)

    def col_copies(a):
        src = xt.at[a, :, :, pl.ds(col_start, 256)]
        make = lambda to, i: pltpu.make_async_remote_copy(
            src_ref=src, dst_ref=cols.at[a], send_sem=ssem.at[col_send[a] + i], recv_sem=rsem.at[col_sem[a]],
            device_id=to, device_id_type=MESH,
        )
        return make(sibling, 0), make(across[0], 0), make(across[1], 1), pltpu.make_async_copy(
            src, cols.at[a], lsem.at[col_here[a]]
        )

    home_holder = jnp.logical_and(holder, at_home)
    far_holder = jnp.logical_and(holder, jnp.logical_not(at_home))

    def send_cols(a):
        home, far0, far1, local = col_copies(a)

        @pl.when(home_holder)
        def _():
            home.start()
            local.start()

        @pl.when(far_holder)
        def _():
            far0.start()
            far1.start()

    def cols_complete(a):
        _, _, _, local = col_copies(a)

        @pl.when(home_holder)
        def _():
            local.wait()

        @pl.when(jnp.logical_not(home_holder))
        def _():
            arrived(cols.at[a], col_sem[a])

    def cols_sent(a):
        home, far0, far1, _ = col_copies(a)

        @pl.when(home_holder)
        def _():
            home.wait_send()

        @pl.when(far_holder)
        def _():
            far0.wait_send()
            far1.wait_send()

    cov_out = (act_o, grad_o)

    def full_cov(a):
        rhs = cols[a].reshape(1024, 256)

        def body(i, _):
            k = pl.ds(pl.multiple_of(i * 256, 256), 256)
            parts = [
                (xt[a, p, :, k].astype(F32) * wcol[:, p : p + 1]).astype(BF) for p in range(8)
            ]
            cov_out[a][k] = lax.dot_general(
                jnp.concatenate(parts, axis=0), rhs, (((0,), (0,)), ((), ())), preferred_element_type=F32
            )
            return 0

        lax.fori_loop(0, 8, body, 0)

    split_row = jnp.clip(PIECE * e - UNITS * tensor, 0, UNITS)
    has_early, has_late = split_row > 0, split_row < UNITS
    blk_out = (hid_o, gg_o, ug_o)

    def block_cov(part):
        row = lax.broadcasted_iota(jnp.int32, (UNITS, 256), 0)

        def body(g, _):
            k = pl.multiple_of(g * 256, 256)

            def product(j, start):
                lhs = jnp.concatenate([sb[j, p] for p in range(8)], axis=1)
                rhs = jnp.concatenate([vw[j, p, pl.ds(start + k, 256)] for p in range(8)], axis=1)
                return lax.dot_general(lhs, rhs, (((1,), (1,)), ((), ())), preferred_element_type=F32)

            @pl.when(jnp.logical_and(has_late, jnp.logical_or(low, 2 * g <= 6 - e)))
            def _():
                for j in arrays_of[part]:
                    blk_out[j][:, pl.ds(k, 256)] = product(j, 1024)

            @pl.when(jnp.logical_and(has_early, jnp.logical_or(jnp.logical_not(low), 2 * g + 1 >= 8 - e)))
            def _():
                for j in arrays_of[part]:
                    blk_out[j][:, pl.ds(k, 256)] = jnp.where(
                        row < split_row, product(j, 0), blk_out[j][:, pl.ds(k, 256)]
                    )

            return 0

        lax.fori_loop(0, 4, body, 0)

    def products_from_neighbour(part):
        row = lax.broadcasted_iota(jnp.int32, (UNITS, 128), 0)
        minor_early = jnp.logical_and(jnp.logical_and(low, e >= 1), has_early)
        minor_late = jnp.logical_and(jnp.logical_and(jnp.logical_not(low), e <= 6), has_late)
        bands = jnp.where(low, split_row, UNITS - split_row) // 32
        start = jnp.where(low, 0, 7 - e)
        stop = jnp.where(low, 8 - e, 8)
        from_row = jnp.where(low, 0, split_row)
        to_row = jnp.where(low, split_row, UNITS)

        def body(col, _):
            sized(bands, 7, lambda n: arrived(res.at[part_of[part], pl.ds(0, 32 * n), pl.ds(0, 128)], res_sem + 8 * part + col))
            at = pl.ds(pl.multiple_of(col * 128, 128), 128)
            here_too = jnp.logical_and(row >= from_row, row < to_row)
            for j in arrays_of[part]:
                blk_out[j][:, at] = jnp.where(here_too, res[j, :, at].astype(F32), blk_out[j][:, at])
            return 0

        @pl.when(jnp.logical_or(minor_early, minor_late))
        def _():
            lax.fori_loop(start, stop, body, 0)

    start_twin(0)
    start_ring(0)
    start_twin(1)
    forward_twin(0)
    start_ring(1)
    forward_twin(1)
    send_packages(0)
    project(0, GATE)
    project(0, UP)
    combine(0, GATE)
    send_packages(1)
    project(0, BACK)
    combine(0, UP)
    combine(0, BACK)
    finish(0, 0)
    forward_packages(0)
    project(1, GATE)
    project(1, UP)
    combine(1, GATE)
    project(2, GATE)
    combine(1, UP)
    project(2, UP)
    combine(2, GATE)
    combine(2, UP)
    finish(0, 1)
    forward_packages(1)
    project(1, BACK)
    project(2, BACK)
    combine(1, BACK)
    combine(2, BACK)
    finish(1, 0)
    finish(2, 0)
    pass_on(0, 0)
    far_packages(0)
    send_cols(0)
    project(3, GATE)
    project(3, UP)
    combine(3, GATE)
    combine(3, UP)
    pass_on(0, 1)
    finish(1, 1)
    finish(2, 1)
    far_packages(1)
    send_cols(1)
    project(3, BACK)
    combine(3, BACK)
    finish(3, 0)
    pass_on(1, 0)
    pass_on(2, 0)
    pass_on(1, 1)
    pass_on(2, 1)
    relay_neighbours(0, 0)
    relay_neighbours(0, 1)
    finish(3, 1)
    cols_complete(0)
    full_cov(0)
    pass_on(3, 0)
    relay_neighbours(1, 0)
    relay_neighbours(2, 0)
    pass_on(3, 1)
    relay_neighbours(3, 0)
    relay_neighbours(1, 1)
    relay_neighbours(2, 1)
    for k in range(CHUNKS):
        units_complete(k, 0)
    products_for_neighbour(0)
    block_cov(0)
    relay_neighbours(3, 1)
    for k in range(CHUNKS):
        units_complete(k, 1)
    products_for_neighbour(1)
    cols_complete(1)
    full_cov(1)
    block_cov(1)
    products_from_neighbour(0)
    products_from_neighbour(1)
    for copy in slot_sent:
        copy.wait_send()
    group_sent("twin", xt.at[0, 0, pl.ds(0, 64)])
    group_sent("ring", xt.at[0, pl.ds(0, 3)])
    group_sent("side", xt.at[0])
    group_sent("far", xt.at[0, pl.ds(0, 4)])
    group_sent("top", tsend)
    group_sent("line", xsend)
    group_sent("cross", sb)
    group_sent("own", sb)
    group_sent("relay", sb)
    for k in range(CHUNKS):
        for part in (0, 1):
            neighbours_sent(k, part)
    for a in (0, 1):
        cols_sent(a)
    products_sent()
    assert (send.used, recv.used, here.used) == (N_SEND, N_RECV, N_LOCAL)


N_SEND, N_RECV, N_LOCAL = 88, 142, 9


def write_out(*refs):
    sources, targets, sems = refs[:5], refs[5:10], refs[10]
    copies = [pltpu.make_async_copy(a, b, sems.at[i]) for i, (a, b) in enumerate(zip(sources, targets))]
    for copy in copies:
        copy.start()
    for copy in copies:
        copy.wait()


def local(tokens, out_grad, gate_weight, up_weight, down_weight, pocket_ids):
    ids = pocket_ids.reshape(8, 128)
    any_spec = pl.BlockSpec(memory_space=pl.ANY)
    vmem = pl.BlockSpec(memory_space=pltpu.VMEM)
    factors = pl.pallas_call(
        kernel,
        out_shape=[
            pltpu.VMEM((2048, 256), F32),
            pltpu.VMEM((2048, 256), F32),
            pltpu.VMEM((UNITS, 1024), F32),
            pltpu.VMEM((UNITS, 1024), F32),
            pltpu.VMEM((UNITS, 1024), F32),
        ],
        in_specs=[any_spec] * 5 + [vmem],
        out_specs=[vmem] * 5,
        scratch_shapes=[
            pltpu.VMEM((2, 8, 128, 2048), BF),
            pltpu.VMEM((2048, SLICE), BF),
            pltpu.VMEM((2048, SLICE), BF),
            pltpu.VMEM((SLICE, 2048), BF),
            pltpu.VMEM((3, 2, 2, UNITS, 256), F32),
            pltpu.VMEM((CHUNKS, 3, 2, UNITS, 256), F32),
            pltpu.VMEM((CHUNKS, 3, UNITS, 256), jnp.int16),
            pltpu.VMEM((CHUNKS, 3, UNITS, 256), jnp.int16),
            pltpu.VMEM((CHUNKS, 3, 1, 256), F32),
            pltpu.VMEM((CHUNKS, 3, 1, 256), F32),
            pltpu.VMEM((3, 8, 2048, 128), BF),
            pltpu.VMEM((3, 8, UNITS, 128), BF),
            pltpu.VMEM((2, 8, 128, 256), BF),
            pltpu.VMEM((3, 3, 128, 256), BF),
            pltpu.VMEM((3, UNITS, 1024), BF),
            pltpu.VMEM((8, 1, 128), F32),
            pltpu.VMEM((128, 8), F32),
            pltpu.SemaphoreType.DMA((N_SEND,)),
            pltpu.SemaphoreType.DMA((N_RECV,)),
            pltpu.SemaphoreType.DMA((N_LOCAL,)),
        ],
        compiler_params=pltpu.CompilerParams(
            collective_id=0, has_side_effects=True, vmem_limit_bytes=52 * MIB
        ),
        name="ekfac_factors",
    )(tokens, out_grad, gate_weight, up_weight, down_weight, ids)
    return pl.pallas_call(
        write_out,
        out_shape=[jax.ShapeDtypeStruct(factor.shape, F32) for factor in factors],
        in_specs=[vmem] * 5,
        out_specs=[any_spec] * 5,
        scratch_shapes=[pltpu.SemaphoreType.DMA((5,))],
        compiler_params=pltpu.CompilerParams(vmem_limit_bytes=4 * MIB),
        name="write_factors",
    )(*(pltpu.with_memory_space_constraint(factor, pltpu.VMEM) for factor in factors))


def solution(mesh):
    return jax.shard_map(
        local,
        mesh=mesh,
        in_specs=(
            P("dp", "tensor"),
            P("dp", "tensor"),
            P("tensor", "dp"),
            P("tensor", "dp"),
            P("dp", "tensor"),
            P(),
        ),
        out_specs=(
            P("tensor", "dp"),
            P("tensor", "dp"),
            P(("dp", "tensor"), None),
            P(("dp", "tensor"), None),
            P(("dp", "tensor"), None),
        ),
        check_vma=False,
    )
```

```python
import functools

import jax
import jax.numpy as jnp
from jax import lax
from jax.experimental import pallas as pl
from jax.experimental.pallas import tpu as pltpu
from jax.sharding import PartitionSpec as P

MESH = pl.DeviceIdType.MESH
POCKETS = 16
BF = jnp.bfloat16
F32 = jnp.float32
MIB = 1 << 20
CHUNKS = 4
UNITS = 224
SLICE = 896
PIECE = 128
GATE, UP, BACK = 0, 1, 2
LEVELS = 32767.0
TINY = 1e-30


def mod4(v):
    return lax.rem(v + 4, 4)


class Sems:
    def __init__(self, ref):
        self.ref, self.used = ref, 0

    def take(self, count=1):
        base = self.used
        self.used += count
        return base


def kernel(
    tok, grd, gate_h, up_h, down_h, ids_ref,
    act_o, grad_o, hid_o, gg_o, ug_o,
    xt, wg, wu, wd, pbuf, rbuf, xsend, xrecv, tsend, trecv, vw, sb, cols, stage, res, wrow, wcol,
    ssem, rsem, lsem,
):
    dp = lax.axis_index("dp")
    tensor = lax.axis_index("tensor")
    xh, y, z = dp // 16, (dp // 4) % 4, dp % 4
    xl, c = tensor // 2, tensor % 2
    e = dp % 8

    def dev(xh_, y_, z_, xl_, c_):
        return {"dp": xh_ * 16 + y_ * 4 + z_, "tensor": xl_ * 2 + c_}

    sibling = dev(xh, y, z, xl, 1 - c)
    partner = dev(xh, y, z, 1 - xl, c)
    twin = dev(1 - xh, y, z, xl, c)
    y_peer = [dev(xh, mod4(y + s), z, xl, c) for s in (1, 2, 3)]
    z_peer = [dev(xh, y, mod4(z + s), xl, c) for s in (1, 2, 3)]
    around = [{"dp": lax.rem(dp + s, 32), "tensor": t} for s in (1, 31) for t in range(4)]
    above, below = ({"dp": lax.rem(dp + s, 32), "tensor": tensor} for s in (1, 31))
    across = [dev(1 - xh, y, z, 1 - xl, k) for k in (0, 1)]

    send, recv, here = Sems(ssem), Sems(rsem), Sems(lsem)
    groups = {}

    def push(src, dst, to, r, group):
        s = groups.setdefault(group, None)
        if s is None:
            s = groups[group] = send.take()
        copy = pltpu.make_async_remote_copy(
            src_ref=src, dst_ref=dst, send_sem=ssem.at[s], recv_sem=rsem.at[r],
            device_id=to, device_id_type=MESH,
        )
        copy.start()
        return copy

    def group_sent(group, ref):
        pltpu.make_async_copy(ref, ref, ssem.at[groups.pop(group)]).wait()

    def arrived(ref, r):
        pltpu.make_async_copy(ref, ref, rsem.at[r]).wait()

    def stay(src, dst):
        copy = pltpu.make_async_copy(src, dst, lsem.at[here.take()])
        copy.start()
        return copy

    shard = (tok, grd)
    pkg_of = (y, 4 + z)
    inner = (xh * 64 + z * 16, xh * 64 + y * 16)
    twin_inner = ((1 - xh) * 64 + z * 16, (1 - xh) * 64 + y * 16)

    def rows16(ref, a, half, start):
        return ref.at[a, pkg_of[half], pl.ds(pl.multiple_of(start, 16), 16)]

    own_copies = [
        [stay(shard[a].at[pl.ds(16 * h, 16)], rows16(xt, a, h, inner[h])) for h in (0, 1)]
        for a in (0, 1)
    ]
    weight_copies = [stay(gate_h, wg), stay(up_h, wu), stay(down_h, wd)]

    def pocket_weights():
        ids = ids_ref[...]
        weights = jnp.zeros((8, 128), F32)
        for k in range(POCKETS):
            member = (ids == k).astype(F32)
            count = jnp.sum(jnp.sum(member, axis=1, keepdims=True), axis=0, keepdims=True)
            weights = weights + member * (1.0 / (POCKETS * count))
        band = lax.broadcasted_iota(jnp.int32, (8, 128), 1) // 16

        def picked(start, at):
            return jnp.where(band == at, pltpu.roll(weights, (16 * (at - start)) % 128, 1), 0.0)

        halves = jnp.zeros((4, 128), F32)
        for at in range(8):
            h = at // 4
            halves = halves + picked(2 * (at % 4), at)[4 * h : 4 * h + 4]
        packages = [halves]
        for k in range(4):
            packages.append(sum(picked(2 * k + 1, at)[at : at + 1] for at in range(8)))
        ordered = jnp.concatenate(packages, axis=0)
        for p in range(8):
            wrow[p] = ordered[p : p + 1]
        wcol[...] = ordered.T

    pocket_weights()

    barrier = pltpu.get_barrier_semaphore()
    greeted = [sibling, partner, twin, *y_peer, *z_peer, *across, *around]
    for peer in greeted:
        pl.semaphore_signal(barrier, inc=1, device_id=peer, device_id_type=MESH)
    pl.semaphore_wait(barrier, len(greeted))

    twin_sem = [[recv.take() for _ in (0, 1)] for _ in (0, 1)]
    ring_sem = [[recv.take() for _ in (0, 1)] for _ in (0, 1)]
    ring_peer = (z_peer, y_peer)
    def start_twin(a):
        for h in (0, 1):
            push(shard[a].at[pl.ds(16 * h, 16)], rows16(xt, a, h, inner[h]), twin, twin_sem[a][h], "twin")

    def start_ring(a):
        for h in (0, 1):
            for peer in ring_peer[h]:
                push(shard[a].at[pl.ds(16 * h, 16)], rows16(xt, a, h, inner[h]), peer, ring_sem[a][h], "ring")

    def forward_twin(a):
        for h in (0, 1):
            piece = rows16(xt, a, h, twin_inner[h])
            arrived(piece, twin_sem[a][h])
            for peer in ring_peer[h]:
                push(piece, piece, peer, ring_sem[a][h], "ring")

    side_peer = ((y_peer[2], y_peer[0]), (z_peer[2], z_peer[0]))
    side_sem = [[[recv.take() for _ in (0, 1)] for _ in (0, 1)] for _ in (0, 1)]
    far_sem = [[[recv.take() for _ in (0, 1)] for _ in (0, 1)] for _ in (0, 1)]
    coord = (y, z)

    def package(h, step):
        return 4 * h + mod4(coord[h] + step)

    def send_packages(a):
        for h in (0, 1):
            own_copies[a][h].wait()
            arrived(xt.at[a, pkg_of[h], pl.ds(0, 96)], ring_sem[a][h])
            whole = xt.at[a, pkg_of[h]]
            for s in (0, 1):
                push(whole, whole, side_peer[h][s], side_sem[a][h][1 - s], "side")

    def forward_packages(a):
        for h in (0, 1):
            for s in (0, 1):
                whole = xt.at[a, package(h, (-1, 1)[s])]
                arrived(whole, side_sem[a][h][s])
                part = xt.at[a, package(h, (-1, 1)[s]), pl.ds(64 * s, 64)]
                push(part, part, side_peer[h][1 - s], far_sem[a][h][s], "far")

    def far_packages(a):
        for h in (0, 1):
            for s in (0, 1):
                arrived(xt.at[a, package(h, 2), pl.ds(64 * s, 64)], far_sem[a][h][s])

    chunk_pkgs = [
        (package(0, 0), package(1, 0)),
        (package(0, -1), package(0, 1)),
        (package(1, -1), package(1, 1)),
        (package(0, 2), package(1, 2)),
    ]

    def pkgs_of(k, y_, z_):
        return [
            (y_, 4 + z_),
            (mod4(y_ - 1), mod4(y_ + 1)),
            (4 + mod4(z_ - 1), 4 + mod4(z_ + 1)),
            (mod4(y_ + 2), 4 + mod4(z_ + 2)),
        ][k]

    core_sem = [[recv.take() for _ in range(3)] for _ in range(CHUNKS)]
    line_sem = [[recv.take() for _ in range(3)] for _ in range(CHUNKS)]
    top_sem = [[recv.take() for _ in range(3)] for _ in range(CHUNKS)]
    slot_of = {}
    slot_sent = [None] * 3
    weights_in = [False] * 3

    def project(k, m):
        if not weights_in[m]:
            weight_copies[m].wait()
            weights_in[m] = True
        slot = len(slot_of) % 3
        assert slot not in busy.values()
        a = 1 if m == BACK else 0
        x = jnp.concatenate([xt[a, chunk_pkgs[k][0]], xt[a, chunk_pkgs[k][1]]], axis=0)
        if m == BACK:
            part = lax.dot_general(wd[...], x, (((1,), (1,)), ((), ())), preferred_element_type=F32)
        else:
            w = (wg, wu)[m]
            part = lax.dot_general(w[...], x, (((0,), (1,)), ((), ())), preferred_element_type=F32)
        if slot_sent[slot] is not None:
            slot_sent[slot].wait_send()
        for i in range(4):
            pbuf[slot, i // 2, i % 2] = part[UNITS * i : UNITS * (i + 1)]
        slot_sent[slot] = push(pbuf.at[slot, :, 1 - c], rbuf.at[k, m], sibling, core_sem[k][m], slot)
        slot_of[k, m] = slot
        busy[k, m] = slot

    busy = {}

    def combine(k, m):
        slot = busy.pop((k, m))
        arrived(rbuf.at[k, m], core_sem[k][m])

        def add(i, top):
            r = pl.ds(pl.multiple_of(i * 32, 32), 32)
            value = rbuf[k, m, 1 - xl, r] + pbuf[slot, 1 - xl, c, r]
            rbuf[k, m, 1 - xl, r] = value
            rbuf[k, m, xl, r] = rbuf[k, m, xl, r] + pbuf[slot, xl, c, r]
            return jnp.maximum(top, jnp.abs(value))

        top = lax.fori_loop(0, UNITS // 32, add, jnp.zeros((32, 256), F32))
        top = jnp.max(top, axis=0, keepdims=True)
        tsend[k, m] = top
        scale = jnp.where(top > TINY, 1.0 / jnp.maximum(top, TINY), 0.0)

        def code(i, _):
            r = pl.ds(pl.multiple_of(i * 32, 32), 32)
            value = rbuf[k, m, 1 - xl, r]
            share = jnp.abs(value) * scale
            root = share * lax.rsqrt(jnp.maximum(share, TINY))
            level = (root * LEVELS + 0.5).astype(jnp.int32)
            xsend[k, m, r] = jnp.where(value < 0, -level, level).astype(jnp.int16)
            return 0

        lax.fori_loop(0, UNITS // 32, code, 0)
        push(tsend.at[k, m], trecv.at[k, m], partner, top_sem[k][m], "top")
        push(xsend.at[k, m], xrecv.at[k, m], partner, line_sem[k][m], "line")

    base = 1024 - PIECE * e

    def rows_of(t):
        return pl.ds(pl.multiple_of(base + UNITS * t, 32), UNITS)

    part_of = (pl.ds(0, 1), pl.ds(1, 2))
    arrays_of = ((0,), (1, 2))
    own_sem, cross_sem, relay_sem = (
        [[recv.take(2) for _ in (0, 1)] for _ in range(CHUNKS)] for _ in range(3)
    )

    def units(part, k, q, t):
        return vw.at[part_of[part], chunk_pkgs[k][q], rows_of(t)]

    def finish(k, part):
        for m in (GATE, UP) if part == 0 else (BACK,):
            arrived(trecv.at[k, m], top_sem[k][m])
            arrived(xrecv.at[k, m], line_sem[k][m])

        def total(m, r):
            root = xrecv[k, m, r].astype(F32) * (1.0 / LEVELS)
            return rbuf[k, m, xl, r] + root * jnp.abs(root) * trecv[k, m]

        def body(i, _):
            r = pl.ds(pl.multiple_of(i * 32, 32), 32)
            gate, up = total(GATE, r), total(UP, r)
            sig = 1.0 / (1.0 + jnp.exp(-gate))
            activated = gate * sig
            if part == 0:
                values = ((0, activated * up),)
            else:
                back = total(BACK, r)
                values = ((1, back * up * sig * (1.0 + gate * (1.0 - sig))), (2, back * activated))
            wr = pl.ds(pl.multiple_of(base + UNITS * tensor + i * 32, 32), 32)
            for j, value in values:
                value = value.astype(BF)
                for q in (0, 1):
                    p = chunk_pkgs[k][q]
                    v = value[:, 128 * q : 128 * (q + 1)]
                    vw[j, p, wr] = v
                    sb[j, p, r] = (v.astype(F32) * wrow[p]).astype(BF)
            return 0

        lax.fori_loop(0, UNITS // 32, body, 0)
        for q in (0, 1):
            mine = units(part, k, q, tensor)
            push(mine, mine, partner, cross_sem[k][part] + q, "cross")
        for q in (0, 1):
            mine = units(part, k, q, tensor)
            push(mine, mine, sibling, own_sem[k][part] + q, "own")

    def relay(k, part, q):
        theirs = units(part, k, q, (1 - xl) * 2 + c)
        arrived(theirs, cross_sem[k][part] + q)
        push(theirs, theirs, sibling, relay_sem[k][part] + q, "relay")

    def package_ready(k, part, q):
        p = jnp.where(q == 0, *chunk_pkgs[k])
        for t, sem in ((xl * 2 + 1 - c, own_sem), ((1 - xl) * 2 + 1 - c, relay_sem)):
            arrived(vw.at[part_of[part], p, rows_of(t)], sem[k][part] + q)

    low = e <= 3
    n_down = jnp.where(e <= 4, e, 0)
    n_up = jnp.where(jnp.logical_and(e >= 3, e <= 6), 7 - e, 0)
    n_near = jnp.where(low, e + 1, 8 - e)
    near_row = jnp.where(low, base + SLICE, 0)
    near_dp = jnp.where(low, dp + 1, dp + 31)
    near_y, near_z = (near_dp // 4) % 4, near_dp % 4
    my_pkg = [jnp.where(c == 0, *chunk_pkgs[k]) for k in range(CHUNKS)]
    near_pkg = [jnp.where(c == 0, *pkgs_of(k, near_y, near_z)) for k in range(CHUNKS)]
    near_sem, near_relay = ([recv.take(2) for _ in range(CHUNKS)] for _ in range(2))
    down_send, up_send, near_send = ([send.take(2) for _ in range(CHUNKS)] for _ in range(3))

    def sized(count, most, f):
        for n in range(1, most + 1):
            pl.when(count == n)(functools.partial(f, n))

    def win(part, p, row, n):
        return vw.at[part_of[part], p, pl.ds(pl.multiple_of(row, PIECE), n * PIECE)]

    def down_copy(k, part, n):
        return pltpu.make_async_remote_copy(
            src_ref=win(part, my_pkg[k], base, n), dst_ref=win(part, my_pkg[k], base + 1024, n),
            send_sem=ssem.at[down_send[k] + part], recv_sem=rsem.at[near_sem[k] + part],
            device_id=below, device_id_type=MESH,
        )

    def up_copy(k, part, n):
        return pltpu.make_async_remote_copy(
            src_ref=win(part, my_pkg[k], base + PIECE * e, n), dst_ref=win(part, my_pkg[k], 0, n),
            send_sem=ssem.at[up_send[k] + part], recv_sem=rsem.at[near_sem[k] + part],
            device_id=above, device_id_type=MESH,
        )

    def near_copy(k, part, n):
        ref = win(part, near_pkg[k], near_row, n)
        return pltpu.make_async_remote_copy(
            src_ref=ref, dst_ref=ref, send_sem=ssem.at[near_send[k] + part], recv_sem=rsem.at[near_relay[k] + part],
            device_id=sibling, device_id_type=MESH,
        )

    def pass_on(k, part):
        for q in (0, 1):
            relay(k, part, q)

            @pl.when(c == q)
            def _():
                package_ready(k, part, q)
                sized(n_down, 4, lambda n: down_copy(k, part, n).start())
                sized(n_up, 4, lambda n: up_copy(k, part, n).start())

    def relay_neighbours(k, part):
        def go(n):
            arrived(win(part, near_pkg[k], near_row, n), near_sem[k] + part)
            near_copy(k, part, n).start()

        sized(n_near, 4, go)

    def units_complete(k, part):
        package_ready(k, part, 1 - c)
        sized(n_near, 4, lambda n: arrived(win(part, near_pkg[k], near_row, n), near_relay[k] + part))

    def neighbours_sent(k, part):
        sized(n_down, 4, lambda n: down_copy(k, part, n).wait_send())
        sized(n_up, 4, lambda n: up_copy(k, part, n).wait_send())
        sized(n_near, 4, lambda n: near_copy(k, part, n).wait_send())

    major = jnp.logical_or(e <= 2, e >= 5)
    n_cols = jnp.where(low, 7 - e, e)
    first_col = jnp.where(low, e, 0)
    res_sem = recv.take(16)
    res_send = send.take(48)
    pair = (tensor, tensor + 4)

    def result_copy(part, i, r, h):
        row = jnp.where(low, 0, PIECE * (e - 1)) + PIECE * i + 32 * r
        owner = row // UNITS
        col = jnp.where(low, 0, 8 - e) + pair[h]
        return pltpu.make_async_remote_copy(
            src_ref=stage.at[part_of[part], i, pl.ds(32 * r, 32), pl.ds(128 * h, 128)],
            dst_ref=res.at[
                part_of[part],
                pl.ds(pl.multiple_of(row - UNITS * owner, 32), 32),
                pl.ds(pl.multiple_of(128 * col, 128), 128),
            ],
            send_sem=ssem.at[res_send + 24 * part + 8 * i + 2 * r + h], recv_sem=rsem.at[res_sem + 8 * part + col],
            device_id={"dp": near_dp % 32, "tensor": owner}, device_id_type=MESH,
        )

    def each_result(part, i, f):
        for h in (0, 1):
            @pl.when(pair[h] < n_cols)
            def _():
                for r in range(4):
                    f(result_copy(part, i, r, h))

    def products_for_neighbour(part):
        def body(i, _):
            rows = pl.ds(pl.multiple_of(near_row + PIECE * i, PIECE), PIECE)
            cols_at = [
                pl.ds(pl.multiple_of(base + PIECE * (first_col + jnp.minimum(piece, n_cols - 1)), PIECE), PIECE)
                for piece in pair
            ]
            for j in arrays_of[part]:
                lhs = jnp.concatenate(
                    [(vw[j, p, rows].astype(F32) * wrow[p]).astype(BF) for p in range(8)], axis=1
                )
                rhs = jnp.concatenate(
                    [jnp.concatenate([vw[j, p, at] for at in cols_at], axis=0) for p in range(8)], axis=1
                )
                stage[j, i] = lax.dot_general(
                    lhs, rhs, (((1,), (1,)), ((), ())), preferred_element_type=F32
                ).astype(BF)
            each_result(part, i, lambda copy: copy.start())
            return 0

        @pl.when(major)
        def _():
            lax.fori_loop(0, n_near, body, 0)

    def products_sent():
        def body(i, _):
            for part in (0, 1):
                each_result(part, i, lambda copy: copy.wait_send())
            return 0

        @pl.when(major)
        def _():
            lax.fori_loop(0, n_near, body, 0)

    col_sem = [recv.take() for _ in (0, 1)]
    col_send = [send.take(2) for _ in (0, 1)]
    col_here = [here.take() for _ in (0, 1)]
    holder = c == y // 2
    at_home = xl == xh
    col_start = pl.multiple_of(e * 256, 256)

    def col_copies(a):
        src = xt.at[a, :, :, pl.ds(col_start, 256)]
        make = lambda to, i: pltpu.make_async_remote_copy(
            src_ref=src, dst_ref=cols.at[a], send_sem=ssem.at[col_send[a] + i], recv_sem=rsem.at[col_sem[a]],
            device_id=to, device_id_type=MESH,
        )
        return make(sibling, 0), make(across[0], 0), make(across[1], 1), pltpu.make_async_copy(
            src, cols.at[a], lsem.at[col_here[a]]
        )

    home_holder = jnp.logical_and(holder, at_home)
    far_holder = jnp.logical_and(holder, jnp.logical_not(at_home))

    def send_cols(a):
        home, far0, far1, local = col_copies(a)

        @pl.when(home_holder)
        def _():
            home.start()
            local.start()

        @pl.when(far_holder)
        def _():
            far0.start()
            far1.start()

    def cols_complete(a):
        _, _, _, local = col_copies(a)

        @pl.when(home_holder)
        def _():
            local.wait()

        @pl.when(jnp.logical_not(home_holder))
        def _():
            arrived(cols.at[a], col_sem[a])

    def cols_sent(a):
        home, far0, far1, _ = col_copies(a)

        @pl.when(home_holder)
        def _():
            home.wait_send()

        @pl.when(far_holder)
        def _():
            far0.wait_send()
            far1.wait_send()

    cov_out = (act_o, grad_o)

    def full_cov(a):
        rhs = cols[a].reshape(1024, 256)

        def body(i, _):
            k = pl.ds(pl.multiple_of(i * 256, 256), 256)
            parts = [
                (xt[a, p, :, k].astype(F32) * wcol[:, p : p + 1]).astype(BF) for p in range(8)
            ]
            cov_out[a][k] = lax.dot_general(
                jnp.concatenate(parts, axis=0), rhs, (((0,), (0,)), ((), ())), preferred_element_type=F32
            )
            return 0

        lax.fori_loop(0, 8, body, 0)

    split_row = jnp.clip(PIECE * e - UNITS * tensor, 0, UNITS)
    has_early, has_late = split_row > 0, split_row < UNITS
    blk_out = (hid_o, gg_o, ug_o)

    def block_cov(part):
        row = lax.broadcasted_iota(jnp.int32, (UNITS, 256), 0)

        def body(g, _):
            k = pl.multiple_of(g * 256, 256)

            def product(j, start):
                lhs = jnp.concatenate([sb[j, p] for p in range(8)], axis=1)
                rhs = jnp.concatenate([vw[j, p, pl.ds(start + k, 256)] for p in range(8)], axis=1)
                return lax.dot_general(lhs, rhs, (((1,), (1,)), ((), ())), preferred_element_type=F32)

            @pl.when(jnp.logical_and(has_late, jnp.logical_or(low, 2 * g <= 6 - e)))
            def _():
                for j in arrays_of[part]:
                    blk_out[j][:, pl.ds(k, 256)] = product(j, 1024)

            @pl.when(jnp.logical_and(has_early, jnp.logical_or(jnp.logical_not(low), 2 * g + 1 >= 8 - e)))
            def _():
                for j in arrays_of[part]:
                    blk_out[j][:, pl.ds(k, 256)] = jnp.where(
                        row < split_row, product(j, 0), blk_out[j][:, pl.ds(k, 256)]
                    )

            return 0

        lax.fori_loop(0, 4, body, 0)

    def products_from_neighbour(part):
        row = lax.broadcasted_iota(jnp.int32, (UNITS, 128), 0)
        minor_early = jnp.logical_and(jnp.logical_and(low, e >= 1), has_early)
        minor_late = jnp.logical_and(jnp.logical_and(jnp.logical_not(low), e <= 6), has_late)
        bands = jnp.where(low, split_row, UNITS - split_row) // 32
        start = jnp.where(low, 0, 7 - e)
        stop = jnp.where(low, 8 - e, 8)
        from_row = jnp.where(low, 0, split_row)
        to_row = jnp.where(low, split_row, UNITS)

        def body(col, _):
            sized(bands, 7, lambda n: arrived(res.at[part_of[part], pl.ds(0, 32 * n), pl.ds(0, 128)], res_sem + 8 * part + col))
            at = pl.ds(pl.multiple_of(col * 128, 128), 128)
            here_too = jnp.logical_and(row >= from_row, row < to_row)
            for j in arrays_of[part]:
                blk_out[j][:, at] = jnp.where(here_too, res[j, :, at].astype(F32), blk_out[j][:, at])
            return 0

        @pl.when(jnp.logical_or(minor_early, minor_late))
        def _():
            lax.fori_loop(start, stop, body, 0)

    start_twin(0)
    start_ring(0)
    start_twin(1)
    forward_twin(0)
    start_ring(1)
    forward_twin(1)
    send_packages(0)
    project(0, GATE)
    project(0, UP)
    combine(0, GATE)
    send_packages(1)
    project(0, BACK)
    combine(0, UP)
    combine(0, BACK)
    finish(0, 0)
    forward_packages(0)
    project(1, GATE)
    project(1, UP)
    combine(1, GATE)
    project(2, GATE)
    combine(1, UP)
    project(2, UP)
    combine(2, GATE)
    combine(2, UP)
    finish(0, 1)
    forward_packages(1)
    project(1, BACK)
    project(2, BACK)
    combine(1, BACK)
    combine(2, BACK)
    finish(1, 0)
    finish(2, 0)
    pass_on(0, 0)
    far_packages(0)
    send_cols(0)
    project(3, GATE)
    project(3, UP)
    combine(3, GATE)
    combine(3, UP)
    pass_on(0, 1)
    finish(1, 1)
    finish(2, 1)
    far_packages(1)
    send_cols(1)
    project(3, BACK)
    combine(3, BACK)
    finish(3, 0)
    pass_on(1, 0)
    pass_on(2, 0)
    pass_on(1, 1)
    pass_on(2, 1)
    relay_neighbours(0, 0)
    relay_neighbours(0, 1)
    finish(3, 1)
    pass_on(3, 0)
    relay_neighbours(1, 0)
    relay_neighbours(2, 0)
    pass_on(3, 1)
    relay_neighbours(3, 0)
    relay_neighbours(1, 1)
    relay_neighbours(2, 1)
    cols_complete(0)
    full_cov(0)
    for k in range(CHUNKS):
        units_complete(k, 0)
    products_for_neighbour(0)
    block_cov(0)
    relay_neighbours(3, 1)
    for k in range(CHUNKS):
        units_complete(k, 1)
    products_for_neighbour(1)
    cols_complete(1)
    full_cov(1)
    block_cov(1)
    products_from_neighbour(0)
    products_from_neighbour(1)
    for copy in slot_sent:
        copy.wait_send()
    group_sent("twin", xt.at[0, 0, pl.ds(0, 64)])
    group_sent("ring", xt.at[0, pl.ds(0, 3)])
    group_sent("side", xt.at[0])
    group_sent("far", xt.at[0, pl.ds(0, 4)])
    group_sent("top", tsend)
    group_sent("line", xsend)
    group_sent("cross", sb)
    group_sent("own", sb)
    group_sent("relay", sb)
    for k in range(CHUNKS):
        for part in (0, 1):
            neighbours_sent(k, part)
    for a in (0, 1):
        cols_sent(a)
    products_sent()
    assert (send.used, recv.used, here.used) == (N_SEND, N_RECV, N_LOCAL)


N_SEND, N_RECV, N_LOCAL = 88, 142, 9


def write_out(*refs):
    sources, targets, sems = refs[:5], refs[5:10], refs[10]
    copies = [pltpu.make_async_copy(a, b, sems.at[i]) for i, (a, b) in enumerate(zip(sources, targets))]
    for copy in copies:
        copy.start()
    for copy in copies:
        copy.wait()


def local(tokens, out_grad, gate_weight, up_weight, down_weight, pocket_ids):
    ids = pocket_ids.reshape(8, 128)
    any_spec = pl.BlockSpec(memory_space=pl.ANY)
    vmem = pl.BlockSpec(memory_space=pltpu.VMEM)
    factors = pl.pallas_call(
        kernel,
        out_shape=[
            pltpu.VMEM((2048, 256), F32),
            pltpu.VMEM((2048, 256), F32),
            pltpu.VMEM((UNITS, 1024), F32),
            pltpu.VMEM((UNITS, 1024), F32),
            pltpu.VMEM((UNITS, 1024), F32),
        ],
        in_specs=[any_spec] * 5 + [vmem],
        out_specs=[vmem] * 5,
        scratch_shapes=[
            pltpu.VMEM((2, 8, 128, 2048), BF),
            pltpu.VMEM((2048, SLICE), BF),
            pltpu.VMEM((2048, SLICE), BF),
            pltpu.VMEM((SLICE, 2048), BF),
            pltpu.VMEM((3, 2, 2, UNITS, 256), F32),
            pltpu.VMEM((CHUNKS, 3, 2, UNITS, 256), F32),
            pltpu.VMEM((CHUNKS, 3, UNITS, 256), jnp.int16),
            pltpu.VMEM((CHUNKS, 3, UNITS, 256), jnp.int16),
            pltpu.VMEM((CHUNKS, 3, 1, 256), F32),
            pltpu.VMEM((CHUNKS, 3, 1, 256), F32),
            pltpu.VMEM((3, 8, 2048, 128), BF),
            pltpu.VMEM((3, 8, UNITS, 128), BF),
            pltpu.VMEM((2, 8, 128, 256), BF),
            pltpu.VMEM((3, 3, 128, 256), BF),
            pltpu.VMEM((3, UNITS, 1024), BF),
            pltpu.VMEM((8, 1, 128), F32),
            pltpu.VMEM((128, 8), F32),
            pltpu.SemaphoreType.DMA((N_SEND,)),
            pltpu.SemaphoreType.DMA((N_RECV,)),
            pltpu.SemaphoreType.DMA((N_LOCAL,)),
        ],
        compiler_params=pltpu.CompilerParams(
            collective_id=0, has_side_effects=True, vmem_limit_bytes=52 * MIB
        ),
        name="ekfac_factors",
    )(tokens, out_grad, gate_weight, up_weight, down_weight, ids)
    return pl.pallas_call(
        write_out,
        out_shape=[jax.ShapeDtypeStruct(factor.shape, F32) for factor in factors],
        in_specs=[vmem] * 5,
        out_specs=[any_spec] * 5,
        scratch_shapes=[pltpu.SemaphoreType.DMA((5,))],
        compiler_params=pltpu.CompilerParams(vmem_limit_bytes=4 * MIB),
        name="write_factors",
    )(*(pltpu.with_memory_space_constraint(factor, pltpu.VMEM) for factor in factors))


def solution(mesh):
    return jax.shard_map(
        local,
        mesh=mesh,
        in_specs=(
            P("dp", "tensor"),
            P("dp", "tensor"),
            P("tensor", "dp"),
            P("tensor", "dp"),
            P("dp", "tensor"),
            P(),
        ),
        out_specs=(
            P("tensor", "dp"),
            P("tensor", "dp"),
            P(("dp", "tensor"), None),
            P(("dp", "tensor"), None),
            P(("dp", "tensor"), None),
        ),
        check_vma=False,
    )
```

```python
import functools

import jax
import jax.numpy as jnp
from jax import lax
from jax.experimental import pallas as pl
from jax.experimental.pallas import tpu as pltpu
from jax.sharding import PartitionSpec as P

MESH = pl.DeviceIdType.MESH
POCKETS = 16
BF = jnp.bfloat16
F32 = jnp.float32
MIB = 1 << 20
CHUNKS = 4
UNITS = 224
SLICE = 896
PIECE = 128
GATE, UP, BACK = 0, 1, 2
LEVELS = 32767.0
TINY = 1e-30


def mod4(v):
    return lax.rem(v + 4, 4)


class Sems:
    def __init__(self, ref):
        self.ref, self.used = ref, 0

    def take(self, count=1):
        base = self.used
        self.used += count
        return base


def kernel(
    tok, grd, gate_h, up_h, down_h, ids_ref,
    act_o, grad_o, hid_o, gg_o, ug_o,
    xt, wg, wu, wd, pbuf, rbuf, xsend, xrecv, tsend, trecv, vw, sb, cols, stage, res, wrow, wcol,
    ssem, rsem, lsem,
):
    dp = lax.axis_index("dp")
    tensor = lax.axis_index("tensor")
    xh, y, z = dp // 16, (dp // 4) % 4, dp % 4
    xl, c = tensor // 2, tensor % 2
    e = dp % 8

    def dev(xh_, y_, z_, xl_, c_):
        return {"dp": xh_ * 16 + y_ * 4 + z_, "tensor": xl_ * 2 + c_}

    sibling = dev(xh, y, z, xl, 1 - c)
    partner = dev(xh, y, z, 1 - xl, c)
    twin = dev(1 - xh, y, z, xl, c)
    y_peer = [dev(xh, mod4(y + s), z, xl, c) for s in (1, 2, 3)]
    z_peer = [dev(xh, y, mod4(z + s), xl, c) for s in (1, 2, 3)]
    around = [{"dp": lax.rem(dp + s, 32), "tensor": t} for s in (1, 31) for t in range(4)]
    above, below = ({"dp": lax.rem(dp + s, 32), "tensor": tensor} for s in (1, 31))
    across = [dev(1 - xh, y, z, 1 - xl, k) for k in (0, 1)]

    send, recv, here = Sems(ssem), Sems(rsem), Sems(lsem)
    groups = {}

    def push(src, dst, to, r, group):
        s = groups.setdefault(group, None)
        if s is None:
            s = groups[group] = send.take()
        copy = pltpu.make_async_remote_copy(
            src_ref=src, dst_ref=dst, send_sem=ssem.at[s], recv_sem=rsem.at[r],
            device_id=to, device_id_type=MESH,
        )
        copy.start()
        return copy

    def group_sent(group, ref):
        pltpu.make_async_copy(ref, ref, ssem.at[groups.pop(group)]).wait()

    def arrived(ref, r):
        pltpu.make_async_copy(ref, ref, rsem.at[r]).wait()

    def stay(src, dst):
        copy = pltpu.make_async_copy(src, dst, lsem.at[here.take()])
        copy.start()
        return copy

    shard = (tok, grd)
    pkg_of = (y, 4 + z)
    inner = (xh * 64 + z * 16, xh * 64 + y * 16)
    twin_inner = ((1 - xh) * 64 + z * 16, (1 - xh) * 64 + y * 16)

    def rows16(ref, a, half, start):
        return ref.at[a, pkg_of[half], pl.ds(pl.multiple_of(start, 16), 16)]

    own_copies = [
        [stay(shard[a].at[pl.ds(16 * h, 16)], rows16(xt, a, h, inner[h])) for h in (0, 1)]
        for a in (0, 1)
    ]
    weight_copies = [stay(gate_h, wg), stay(up_h, wu), stay(down_h, wd)]

    def pocket_weights():
        ids = ids_ref[...]
        weights = jnp.zeros((8, 128), F32)
        for k in range(POCKETS):
            member = (ids == k).astype(F32)
            count = jnp.sum(jnp.sum(member, axis=1, keepdims=True), axis=0, keepdims=True)
            weights = weights + member * (1.0 / (POCKETS * count))
        band = lax.broadcasted_iota(jnp.int32, (8, 128), 1) // 16

        def picked(start, at):
            return jnp.where(band == at, pltpu.roll(weights, (16 * (at - start)) % 128, 1), 0.0)

        halves = jnp.zeros((4, 128), F32)
        for at in range(8):
            h = at // 4
            halves = halves + picked(2 * (at % 4), at)[4 * h : 4 * h + 4]
        packages = [halves]
        for k in range(4):
            packages.append(sum(picked(2 * k + 1, at)[at : at + 1] for at in range(8)))
        ordered = jnp.concatenate(packages, axis=0)
        for p in range(8):
            wrow[p] = ordered[p : p + 1]
        wcol[...] = ordered.T

    pocket_weights()

    barrier = pltpu.get_barrier_semaphore()
    greeted = [sibling, partner, twin, *y_peer, *z_peer, *across, *around]
    for peer in greeted:
        pl.semaphore_signal(barrier, inc=1, device_id=peer, device_id_type=MESH)
    pl.semaphore_wait(barrier, len(greeted))

    twin_sem = [[recv.take() for _ in (0, 1)] for _ in (0, 1)]
    ring_sem = [[recv.take() for _ in (0, 1)] for _ in (0, 1)]
    ring_peer = (z_peer, y_peer)
    def start_twin(a):
        for h in (0, 1):
            push(shard[a].at[pl.ds(16 * h, 16)], rows16(xt, a, h, inner[h]), twin, twin_sem[a][h], "twin")

    def start_ring(a):
        for h in (0, 1):
            for peer in ring_peer[h]:
                push(shard[a].at[pl.ds(16 * h, 16)], rows16(xt, a, h, inner[h]), peer, ring_sem[a][h], "ring")

    def forward_twin(a):
        for h in (0, 1):
            piece = rows16(xt, a, h, twin_inner[h])
            arrived(piece, twin_sem[a][h])
            for peer in ring_peer[h]:
                push(piece, piece, peer, ring_sem[a][h], "ring")

    side_peer = ((y_peer[2], y_peer[0]), (z_peer[2], z_peer[0]))
    side_sem = [[[recv.take() for _ in (0, 1)] for _ in (0, 1)] for _ in (0, 1)]
    far_sem = [[[recv.take() for _ in (0, 1)] for _ in (0, 1)] for _ in (0, 1)]
    coord = (y, z)

    def package(h, step):
        return 4 * h + mod4(coord[h] + step)

    def send_packages(a):
        for h in (0, 1):
            own_copies[a][h].wait()
            arrived(xt.at[a, pkg_of[h], pl.ds(0, 96)], ring_sem[a][h])
            whole = xt.at[a, pkg_of[h]]
            for s in (0, 1):
                push(whole, whole, side_peer[h][s], side_sem[a][h][1 - s], "side")

    def forward_packages(a):
        for h in (0, 1):
            for s in (0, 1):
                whole = xt.at[a, package(h, (-1, 1)[s])]
                arrived(whole, side_sem[a][h][s])
                part = xt.at[a, package(h, (-1, 1)[s]), pl.ds(64 * s, 64)]
                push(part, part, side_peer[h][1 - s], far_sem[a][h][s], "far")

    def far_packages(a):
        for h in (0, 1):
            for s in (0, 1):
                arrived(xt.at[a, package(h, 2), pl.ds(64 * s, 64)], far_sem[a][h][s])

    chunk_pkgs = [
        (package(0, 0), package(1, 0)),
        (package(0, -1), package(0, 1)),
        (package(1, -1), package(1, 1)),
        (package(0, 2), package(1, 2)),
    ]

    def pkgs_of(k, y_, z_):
        return [
            (y_, 4 + z_),
            (mod4(y_ - 1), mod4(y_ + 1)),
            (4 + mod4(z_ - 1), 4 + mod4(z_ + 1)),
            (mod4(y_ + 2), 4 + mod4(z_ + 2)),
        ][k]

    core_sem = [[recv.take() for _ in range(3)] for _ in range(CHUNKS)]
    line_sem = [[recv.take() for _ in range(3)] for _ in range(CHUNKS)]
    top_sem = [[recv.take() for _ in range(3)] for _ in range(CHUNKS)]
    slot_of = {}
    slot_sent = [None] * 3
    weights_in = [False] * 3

    def project(k, m):
        if not weights_in[m]:
            weight_copies[m].wait()
            weights_in[m] = True
        slot = len(slot_of) % 3
        assert slot not in busy.values()
        a = 1 if m == BACK else 0
        x = jnp.concatenate([xt[a, chunk_pkgs[k][0]], xt[a, chunk_pkgs[k][1]]], axis=0)
        if m == BACK:
            part = lax.dot_general(wd[...], x, (((1,), (1,)), ((), ())), preferred_element_type=F32)
        else:
            w = (wg, wu)[m]
            part = lax.dot_general(w[...], x, (((0,), (1,)), ((), ())), preferred_element_type=F32)
        if slot_sent[slot] is not None:
            slot_sent[slot].wait_send()
        for i in range(4):
            pbuf[slot, i // 2, i % 2] = part[UNITS * i : UNITS * (i + 1)]
        slot_sent[slot] = push(pbuf.at[slot, :, 1 - c], rbuf.at[k, m], sibling, core_sem[k][m], slot)
        slot_of[k, m] = slot
        busy[k, m] = slot

    busy = {}

    def combine(k, m):
        slot = busy.pop((k, m))
        arrived(rbuf.at[k, m], core_sem[k][m])

        def add(i, top):
            r = pl.ds(pl.multiple_of(i * 32, 32), 32)
            value = rbuf[k, m, 1 - xl, r] + pbuf[slot, 1 - xl, c, r]
            rbuf[k, m, 1 - xl, r] = value
            rbuf[k, m, xl, r] = rbuf[k, m, xl, r] + pbuf[slot, xl, c, r]
            return jnp.maximum(top, jnp.abs(value))

        top = lax.fori_loop(0, UNITS // 32, add, jnp.zeros((32, 256), F32))
        top = jnp.max(top, axis=0, keepdims=True)
        tsend[k, m] = top
        scale = jnp.where(top > TINY, 1.0 / jnp.maximum(top, TINY), 0.0)

        def code(i, _):
            r = pl.ds(pl.multiple_of(i * 32, 32), 32)
            value = rbuf[k, m, 1 - xl, r]
            share = jnp.abs(value) * scale
            root = share * lax.rsqrt(jnp.maximum(share, TINY))
            level = (root * LEVELS + 0.5).astype(jnp.int32)
            xsend[k, m, r] = jnp.where(value < 0, -level, level).astype(jnp.int16)
            return 0

        lax.fori_loop(0, UNITS // 32, code, 0)
        push(tsend.at[k, m], trecv.at[k, m], partner, top_sem[k][m], "top")
        push(xsend.at[k, m], xrecv.at[k, m], partner, line_sem[k][m], "line")

    base = 1024 - PIECE * e

    def rows_of(t):
        return pl.ds(pl.multiple_of(base + UNITS * t, 32), UNITS)

    part_of = (pl.ds(0, 1), pl.ds(1, 2))
    arrays_of = ((0,), (1, 2))
    own_sem, cross_sem, relay_sem = (
        [[recv.take(2) for _ in (0, 1)] for _ in range(CHUNKS)] for _ in range(3)
    )

    def units(part, k, q, t):
        return vw.at[part_of[part], chunk_pkgs[k][q], rows_of(t)]

    def finish(k, part):
        for m in (GATE, UP) if part == 0 else (BACK,):
            arrived(trecv.at[k, m], top_sem[k][m])
            arrived(xrecv.at[k, m], line_sem[k][m])

        def total(m, r):
            root = xrecv[k, m, r].astype(F32) * (1.0 / LEVELS)
            return rbuf[k, m, xl, r] + root * jnp.abs(root) * trecv[k, m]

        def body(i, _):
            r = pl.ds(pl.multiple_of(i * 32, 32), 32)
            gate, up = total(GATE, r), total(UP, r)
            sig = 1.0 / (1.0 + jnp.exp(-gate))
            activated = gate * sig
            if part == 0:
                values = ((0, activated * up),)
            else:
                back = total(BACK, r)
                values = ((1, back * up * sig * (1.0 + gate * (1.0 - sig))), (2, back * activated))
            wr = pl.ds(pl.multiple_of(base + UNITS * tensor + i * 32, 32), 32)
            for j, value in values:
                value = value.astype(BF)
                for q in (0, 1):
                    p = chunk_pkgs[k][q]
                    v = value[:, 128 * q : 128 * (q + 1)]
                    vw[j, p, wr] = v
                    sb[j, p, r] = (v.astype(F32) * wrow[p]).astype(BF)
            return 0

        lax.fori_loop(0, UNITS // 32, body, 0)
        for q in (0, 1):
            mine = units(part, k, q, tensor)
            push(mine, mine, partner, cross_sem[k][part] + q, "cross")
        for q in (0, 1):
            mine = units(part, k, q, tensor)
            push(mine, mine, sibling, own_sem[k][part] + q, "own")

    def relay(k, part, q):
        theirs = units(part, k, q, (1 - xl) * 2 + c)
        arrived(theirs, cross_sem[k][part] + q)
        push(theirs, theirs, sibling, relay_sem[k][part] + q, "relay")

    def package_ready(k, part, q):
        p = jnp.where(q == 0, *chunk_pkgs[k])
        for t, sem in ((xl * 2 + 1 - c, own_sem), ((1 - xl) * 2 + 1 - c, relay_sem)):
            arrived(vw.at[part_of[part], p, rows_of(t)], sem[k][part] + q)

    low = e <= 3
    n_down = jnp.where(e <= 4, e, 0)
    n_up = jnp.where(jnp.logical_and(e >= 3, e <= 6), 7 - e, 0)
    n_near = jnp.where(low, e + 1, 8 - e)
    near_row = jnp.where(low, base + SLICE, 0)
    near_dp = jnp.where(low, dp + 1, dp + 31)
    near_y, near_z = (near_dp // 4) % 4, near_dp % 4
    my_pkg = [jnp.where(c == 0, *chunk_pkgs[k]) for k in range(CHUNKS)]
    near_pkg = [jnp.where(c == 0, *pkgs_of(k, near_y, near_z)) for k in range(CHUNKS)]
    near_sem, near_relay = ([recv.take(2) for _ in range(CHUNKS)] for _ in range(2))
    down_send, up_send, near_send = ([send.take(2) for _ in range(CHUNKS)] for _ in range(3))

    def sized(count, most, f):
        for n in range(1, most + 1):
            pl.when(count == n)(functools.partial(f, n))

    def win(part, p, row, n):
        return vw.at[part_of[part], p, pl.ds(pl.multiple_of(row, PIECE), n * PIECE)]

    def down_copy(k, part, n):
        return pltpu.make_async_remote_copy(
            src_ref=win(part, my_pkg[k], base, n), dst_ref=win(part, my_pkg[k], base + 1024, n),
            send_sem=ssem.at[down_send[k] + part], recv_sem=rsem.at[near_sem[k] + part],
            device_id=below, device_id_type=MESH,
        )

    def up_copy(k, part, n):
        return pltpu.make_async_remote_copy(
            src_ref=win(part, my_pkg[k], base + PIECE * e, n), dst_ref=win(part, my_pkg[k], 0, n),
            send_sem=ssem.at[up_send[k] + part], recv_sem=rsem.at[near_sem[k] + part],
            device_id=above, device_id_type=MESH,
        )

    def near_copy(k, part, n):
        ref = win(part, near_pkg[k], near_row, n)
        return pltpu.make_async_remote_copy(
            src_ref=ref, dst_ref=ref, send_sem=ssem.at[near_send[k] + part], recv_sem=rsem.at[near_relay[k] + part],
            device_id=sibling, device_id_type=MESH,
        )

    def pass_on(k, part):
        for q in (0, 1):
            relay(k, part, q)

            @pl.when(c == q)
            def _():
                package_ready(k, part, q)
                sized(n_down, 4, lambda n: down_copy(k, part, n).start())
                sized(n_up, 4, lambda n: up_copy(k, part, n).start())

    def relay_neighbours(k, part):
        def go(n):
            arrived(win(part, near_pkg[k], near_row, n), near_sem[k] + part)
            near_copy(k, part, n).start()

        sized(n_near, 4, go)

    def units_complete(k, part):
        package_ready(k, part, 1 - c)
        sized(n_near, 4, lambda n: arrived(win(part, near_pkg[k], near_row, n), near_relay[k] + part))

    def neighbours_sent(k, part):
        sized(n_down, 4, lambda n: down_copy(k, part, n).wait_send())
        sized(n_up, 4, lambda n: up_copy(k, part, n).wait_send())
        sized(n_near, 4, lambda n: near_copy(k, part, n).wait_send())

    major = jnp.logical_or(e <= 2, e >= 5)
    n_cols = jnp.where(low, 7 - e, e)
    first_col = jnp.where(low, e, 0)
    res_sem = recv.take(16)
    res_send = send.take(48)
    pair = (tensor, tensor + 4)

    def result_copy(part, i, r, h):
        row = jnp.where(low, 0, PIECE * (e - 1)) + PIECE * i + 32 * r
        owner = row // UNITS
        col = jnp.where(low, 0, 8 - e) + pair[h]
        return pltpu.make_async_remote_copy(
            src_ref=stage.at[part_of[part], i, pl.ds(32 * r, 32), pl.ds(128 * h, 128)],
            dst_ref=res.at[
                part_of[part],
                pl.ds(pl.multiple_of(row - UNITS * owner, 32), 32),
                pl.ds(pl.multiple_of(128 * col, 128), 128),
            ],
            send_sem=ssem.at[res_send + 24 * part + 8 * i + 2 * r + h], recv_sem=rsem.at[res_sem + 8 * part + col],
            device_id={"dp": near_dp % 32, "tensor": owner}, device_id_type=MESH,
        )

    def each_result(part, i, f):
        for h in (0, 1):
            @pl.when(pair[h] < n_cols)
            def _():
                for r in range(4):
                    f(result_copy(part, i, r, h))

    def products_for_neighbour(part):
        def body(i, _):
            rows = pl.ds(pl.multiple_of(near_row + PIECE * i, PIECE), PIECE)
            cols_at = [
                pl.ds(pl.multiple_of(base + PIECE * (first_col + jnp.minimum(piece, n_cols - 1)), PIECE), PIECE)
                for piece in pair
            ]
            for j in arrays_of[part]:
                lhs = jnp.concatenate(
                    [(vw[j, p, rows].astype(F32) * wrow[p]).astype(BF) for p in range(8)], axis=1
                )
                rhs = jnp.concatenate(
                    [jnp.concatenate([vw[j, p, at] for at in cols_at], axis=0) for p in range(8)], axis=1
                )
                stage[j, i] = lax.dot_general(
                    lhs, rhs, (((1,), (1,)), ((), ())), preferred_element_type=F32
                ).astype(BF)
            each_result(part, i, lambda copy: copy.start())
            return 0

        @pl.when(major)
        def _():
            lax.fori_loop(0, n_near, body, 0)

    def products_sent():
        def body(i, _):
            for part in (0, 1):
                each_result(part, i, lambda copy: copy.wait_send())
            return 0

        @pl.when(major)
        def _():
            lax.fori_loop(0, n_near, body, 0)

    col_sem = [recv.take() for _ in (0, 1)]
    col_send = [send.take(2) for _ in (0, 1)]
    col_here = [here.take() for _ in (0, 1)]
    holder = c == y // 2
    at_home = xl == xh
    col_start = pl.multiple_of(e * 256, 256)

    def col_copies(a):
        src = xt.at[a, :, :, pl.ds(col_start, 256)]
        make = lambda to, i: pltpu.make_async_remote_copy(
            src_ref=src, dst_ref=cols.at[a], send_sem=ssem.at[col_send[a] + i], recv_sem=rsem.at[col_sem[a]],
            device_id=to, device_id_type=MESH,
        )
        return make(sibling, 0), make(across[0], 0), make(across[1], 1), pltpu.make_async_copy(
            src, cols.at[a], lsem.at[col_here[a]]
        )

    home_holder = jnp.logical_and(holder, at_home)
    far_holder = jnp.logical_and(holder, jnp.logical_not(at_home))

    def send_cols(a):
        home, far0, far1, local = col_copies(a)

        @pl.when(home_holder)
        def _():
            home.start()
            local.start()

        @pl.when(far_holder)
        def _():
            far0.start()
            far1.start()

    def cols_complete(a):
        _, _, _, local = col_copies(a)

        @pl.when(home_holder)
        def _():
            local.wait()

        @pl.when(jnp.logical_not(home_holder))
        def _():
            arrived(cols.at[a], col_sem[a])

    def cols_sent(a):
        home, far0, far1, _ = col_copies(a)

        @pl.when(home_holder)
        def _():
            home.wait_send()

        @pl.when(far_holder)
        def _():
            far0.wait_send()
            far1.wait_send()

    cov_out = (act_o, grad_o)

    def full_cov(a):
        rhs = cols[a].reshape(1024, 256)

        def body(i, _):
            k = pl.ds(pl.multiple_of(i * 256, 256), 256)
            parts = [
                (xt[a, p, :, k].astype(F32) * wcol[:, p : p + 1]).astype(BF) for p in range(8)
            ]
            cov_out[a][k] = lax.dot_general(
                jnp.concatenate(parts, axis=0), rhs, (((0,), (0,)), ((), ())), preferred_element_type=F32
            )
            return 0

        lax.fori_loop(0, 8, body, 0)

    split_row = jnp.clip(PIECE * e - UNITS * tensor, 0, UNITS)
    has_early, has_late = split_row > 0, split_row < UNITS
    blk_out = (hid_o, gg_o, ug_o)

    def block_cov(part):
        row = lax.broadcasted_iota(jnp.int32, (UNITS, 256), 0)

        def body(g, _):
            k = pl.multiple_of(g * 256, 256)

            def product(j, start):
                lhs = jnp.concatenate([sb[j, p] for p in range(8)], axis=1)
                rhs = jnp.concatenate([vw[j, p, pl.ds(start + k, 256)] for p in range(8)], axis=1)
                return lax.dot_general(lhs, rhs, (((1,), (1,)), ((), ())), preferred_element_type=F32)

            @pl.when(jnp.logical_and(has_late, jnp.logical_or(low, 2 * g <= 6 - e)))
            def _():
                for j in arrays_of[part]:
                    blk_out[j][:, pl.ds(k, 256)] = product(j, 1024)

            @pl.when(jnp.logical_and(has_early, jnp.logical_or(jnp.logical_not(low), 2 * g + 1 >= 8 - e)))
            def _():
                for j in arrays_of[part]:
                    blk_out[j][:, pl.ds(k, 256)] = jnp.where(
                        row < split_row, product(j, 0), blk_out[j][:, pl.ds(k, 256)]
                    )

            return 0

        lax.fori_loop(0, 4, body, 0)

    def products_from_neighbour(part):
        row = lax.broadcasted_iota(jnp.int32, (UNITS, 128), 0)
        minor_early = jnp.logical_and(jnp.logical_and(low, e >= 1), has_early)
        minor_late = jnp.logical_and(jnp.logical_and(jnp.logical_not(low), e <= 6), has_late)
        bands = jnp.where(low, split_row, UNITS - split_row) // 32
        start = jnp.where(low, 0, 7 - e)
        stop = jnp.where(low, 8 - e, 8)
        from_row = jnp.where(low, 0, split_row)
        to_row = jnp.where(low, split_row, UNITS)

        def body(col, _):
            sized(bands, 7, lambda n: arrived(res.at[part_of[part], pl.ds(0, 32 * n), pl.ds(0, 128)], res_sem + 8 * part + col))
            at = pl.ds(pl.multiple_of(col * 128, 128), 128)
            here_too = jnp.logical_and(row >= from_row, row < to_row)
            for j in arrays_of[part]:
                blk_out[j][:, at] = jnp.where(here_too, res[j, :, at].astype(F32), blk_out[j][:, at])
            return 0

        @pl.when(jnp.logical_or(minor_early, minor_late))
        def _():
            lax.fori_loop(start, stop, body, 0)

    start_twin(0)
    start_ring(0)
    start_twin(1)
    forward_twin(0)
    start_ring(1)
    forward_twin(1)
    send_packages(0)
    project(0, GATE)
    project(0, UP)
    combine(0, GATE)
    send_packages(1)
    project(0, BACK)
    combine(0, UP)
    combine(0, BACK)
    finish(0, 0)
    forward_packages(0)
    project(1, GATE)
    finish(0, 1)
    project(1, UP)
    combine(1, GATE)
    project(2, GATE)
    combine(1, UP)
    project(2, UP)
    combine(2, GATE)
    combine(2, UP)
    forward_packages(1)
    project(1, BACK)
    project(2, BACK)
    combine(1, BACK)
    combine(2, BACK)
    finish(1, 0)
    finish(2, 0)
    pass_on(0, 0)
    far_packages(0)
    send_cols(0)
    project(3, GATE)
    project(3, UP)
    combine(3, GATE)
    combine(3, UP)
    pass_on(0, 1)
    finish(1, 1)
    finish(2, 1)
    far_packages(1)
    send_cols(1)
    project(3, BACK)
    combine(3, BACK)
    finish(3, 0)
    pass_on(1, 0)
    pass_on(2, 0)
    pass_on(1, 1)
    pass_on(2, 1)
    relay_neighbours(0, 0)
    relay_neighbours(0, 1)
    finish(3, 1)
    pass_on(3, 0)
    relay_neighbours(1, 0)
    relay_neighbours(2, 0)
    pass_on(3, 1)
    relay_neighbours(3, 0)
    relay_neighbours(1, 1)
    relay_neighbours(2, 1)
    cols_complete(0)
    full_cov(0)
    for k in range(CHUNKS):
        units_complete(k, 0)
    products_for_neighbour(0)
    block_cov(0)
    relay_neighbours(3, 1)
    for k in range(CHUNKS):
        units_complete(k, 1)
    products_for_neighbour(1)
    cols_complete(1)
    full_cov(1)
    block_cov(1)
    products_from_neighbour(0)
    products_from_neighbour(1)
    for copy in slot_sent:
        copy.wait_send()
    group_sent("twin", xt.at[0, 0, pl.ds(0, 64)])
    group_sent("ring", xt.at[0, pl.ds(0, 3)])
    group_sent("side", xt.at[0])
    group_sent("far", xt.at[0, pl.ds(0, 4)])
    group_sent("top", tsend)
    group_sent("line", xsend)
    group_sent("cross", sb)
    group_sent("own", sb)
    group_sent("relay", sb)
    for k in range(CHUNKS):
        for part in (0, 1):
            neighbours_sent(k, part)
    for a in (0, 1):
        cols_sent(a)
    products_sent()
    assert (send.used, recv.used, here.used) == (N_SEND, N_RECV, N_LOCAL)


N_SEND, N_RECV, N_LOCAL = 88, 142, 9


def write_out(*refs):
    sources, targets, sems = refs[:5], refs[5:10], refs[10]
    copies = [pltpu.make_async_copy(a, b, sems.at[i]) for i, (a, b) in enumerate(zip(sources, targets))]
    for copy in copies:
        copy.start()
    for copy in copies:
        copy.wait()


def local(tokens, out_grad, gate_weight, up_weight, down_weight, pocket_ids):
    ids = pocket_ids.reshape(8, 128)
    any_spec = pl.BlockSpec(memory_space=pl.ANY)
    vmem = pl.BlockSpec(memory_space=pltpu.VMEM)
    factors = pl.pallas_call(
        kernel,
        out_shape=[
            pltpu.VMEM((2048, 256), F32),
            pltpu.VMEM((2048, 256), F32),
            pltpu.VMEM((UNITS, 1024), F32),
            pltpu.VMEM((UNITS, 1024), F32),
            pltpu.VMEM((UNITS, 1024), F32),
        ],
        in_specs=[any_spec] * 5 + [vmem],
        out_specs=[vmem] * 5,
        scratch_shapes=[
            pltpu.VMEM((2, 8, 128, 2048), BF),
            pltpu.VMEM((2048, SLICE), BF),
            pltpu.VMEM((2048, SLICE), BF),
            pltpu.VMEM((SLICE, 2048), BF),
            pltpu.VMEM((3, 2, 2, UNITS, 256), F32),
            pltpu.VMEM((CHUNKS, 3, 2, UNITS, 256), F32),
            pltpu.VMEM((CHUNKS, 3, UNITS, 256), jnp.int16),
            pltpu.VMEM((CHUNKS, 3, UNITS, 256), jnp.int16),
            pltpu.VMEM((CHUNKS, 3, 1, 256), F32),
            pltpu.VMEM((CHUNKS, 3, 1, 256), F32),
            pltpu.VMEM((3, 8, 2048, 128), BF),
            pltpu.VMEM((3, 8, UNITS, 128), BF),
            pltpu.VMEM((2, 8, 128, 256), BF),
            pltpu.VMEM((3, 3, 128, 256), BF),
            pltpu.VMEM((3, UNITS, 1024), BF),
            pltpu.VMEM((8, 1, 128), F32),
            pltpu.VMEM((128, 8), F32),
            pltpu.SemaphoreType.DMA((N_SEND,)),
            pltpu.SemaphoreType.DMA((N_RECV,)),
            pltpu.SemaphoreType.DMA((N_LOCAL,)),
        ],
        compiler_params=pltpu.CompilerParams(
            collective_id=0, has_side_effects=True, vmem_limit_bytes=52 * MIB
        ),
        name="ekfac_factors",
    )(tokens, out_grad, gate_weight, up_weight, down_weight, ids)
    return pl.pallas_call(
        write_out,
        out_shape=[jax.ShapeDtypeStruct(factor.shape, F32) for factor in factors],
        in_specs=[vmem] * 5,
        out_specs=[any_spec] * 5,
        scratch_shapes=[pltpu.SemaphoreType.DMA((5,))],
        compiler_params=pltpu.CompilerParams(vmem_limit_bytes=4 * MIB),
        name="write_factors",
    )(*(pltpu.with_memory_space_constraint(factor, pltpu.VMEM) for factor in factors))


def solution(mesh):
    return jax.shard_map(
        local,
        mesh=mesh,
        in_specs=(
            P("dp", "tensor"),
            P("dp", "tensor"),
            P("tensor", "dp"),
            P("tensor", "dp"),
            P("dp", "tensor"),
            P(),
        ),
        out_specs=(
            P("tensor", "dp"),
            P("tensor", "dp"),
            P(("dp", "tensor"), None),
            P(("dp", "tensor"), None),
            P(("dp", "tensor"), None),
        ),
        check_vma=False,
    )
```
